512 devices in a mesh: section: 4 (over x), dp: 16 (over z), mp: 8 (over y, core).
Axes of the slice: x: 4, y: 4, z: 16, core: 2. Of those that a mesh axis runs over, the one named last changes fastest.
Arguments:
- images: bfloat16 [32, 2, 8, 12, 768], P('dp'), may hold values from -6 to 6
- token_grads: bfloat16 [32, 2, 8, 12, 768], P('dp'), may hold values from -0.119628906 to 0.119628906
- counts: int32 [32], P('dp'), may hold values from 1 to 2
- dw_kernel: float32 [4, 7, 7, 768], P('section'), may hold values from -0.875 to 0.875
- ln_gain: float32 [4, 768], P('section'), may hold values from 0.5 to 1.5
- w_in: bfloat16 [4, 768, 3072], P('section', None, 'mp'), may hold values from -0.21875 to 0.21875
- w_out: bfloat16 [4, 3072, 768], P('section', 'mp'), may hold values from -0.109375 to 0.109375
- layer_scale: float32 [4, 768], P('section'), may hold values from 0.3 to 1.5
Outputs:
- grad_in: bfloat16 [4, 768, 3072], P('section', 'dp', 'mp')
- grad_out_t: bfloat16 [4, 768, 3072], P('section', 'dp', 'mp')
The draws below stay inside these ranges and needn't reach their ends.
Inputs may be any that keep to these rules, and one draw needn't show every extreme that they name: Each sample has at least one image; its first counts images are live.
All inputs are finite; a program needn't handle non-finite values.
Results may differ from the reference program's by a relative error of at most 0.04.
Values may be sent and summed in bfloat16 or wider, within the bound.
No kernel may reach another device: no remote copies, remote signals or barrier semaphores. Data moves between devices by JAX's collectives and lax.ppermute only.
A program may use at most 128 MiB of HBM per device.

```python
import math
import jax
import jax.numpy as jnp
from jax import lax

C = 768
FF = 3072
TAPS = 7
IMGS = 2
ROWS = 8
COLS = 12
MICRO = 2
SECTIONS = 4
BATCH = 32
N_DP = 16
N_MP = 8


def touch_ends(entries, own_key, smallest, top_value):
    longest = entries.shape.index(max(entries.shape))
    spots = []
    for shift in (0, 1):
        where = [jax.random.randint(jax.random.fold_in(own_key, axis), (), 0, length) for axis, length in enumerate(entries.shape)]
        where[longest] = (where[longest] + shift) % entries.shape[longest]
        spots.append(tuple(where))
    return entries.at[spots[0]].set(smallest).at[spots[1]].set(top_value)


def block_scale(stream_key, shape, shards, least, largest):
    factor_of = 1.0
    for dim, shards_of in shards:
        draws = jax.random.uniform(jax.random.fold_in(jax.random.fold_in(stream_key, 6), dim), (shards_of,), jnp.float32, least / len(shards), largest / len(shards))
        factor_of = factor_of * jnp.repeat(jnp.exp(draws), shape[dim] // shards_of).reshape((-1,) + (1,) * (len(shape) - 1 - dim))
    return factor_of


def centred(stream_key, extent, scale, limit, shards=(), kind=jnp.bfloat16):
    result = jax.random.normal(stream_key, extent, jnp.float32) * scale
    if len(shards) > 0:
        result = block_scale(stream_key, extent, shards, -0.22, 0.18) * result
    return jnp.clip(result, min=-limit, max=limit).astype(kind)


def setup_inputs(seed: int = 0) -> dict:
    splits = jax.random.split(jax.random.key(seed), 9)
    images = centred(splits[0], (BATCH, IMGS, ROWS, COLS, C), 1.0, 6.0, ((0, 16),))
    token_grads = centred(splits[1], (BATCH, IMGS, ROWS, COLS, C), 0.02, 0.119628906, ((0, 16),))
    counts = touch_ends(jax.random.randint(splits[2], (BATCH,), 1, IMGS + 1), jax.random.fold_in(splits[2], 1), 1, IMGS).astype(jnp.int32)
    dw_kernel = centred(splits[3], (SECTIONS, TAPS, TAPS, C), (TAPS * TAPS) ** -0.5, 0.875, ((0, 4),), jnp.float32)
    ln_gain = jnp.clip(1.0 + 0.1 * jax.random.normal(splits[4], (SECTIONS, C), jnp.float32), 0.5, 1.5)
    w_in = centred(splits[5], (SECTIONS, C, FF), C ** -0.5, 0.21875, ((0, 4), (2, 8)))
    w_out = centred(splits[6], (SECTIONS, FF, C), FF ** -0.5, 0.109375, ((0, 4), (1, 8)))
    layer_scale = jnp.clip(jnp.exp(math.log(1.5) - 1.60943787 * jax.random.uniform(splits[7], (SECTIONS, C), jnp.float32) ** block_scale(splits[7], (SECTIONS, C), ((0, 4),), -0.2, 0.2)), 0.3, 1.5)
    return dict(images=images, token_grads=token_grads, counts=counts, dw_kernel=dw_kernel, ln_gain=ln_gain, w_in=w_in, w_out=w_out, layer_scale=layer_scale)


def mix_in(block_in, kernel, gain):
    values = block_in.astype(jnp.float32)
    rows = values.shape[-3]
    cols = values.shape[-2]
    widths = [(0, 0)] * (values.ndim - 3) + [(3, 3), (3, 3), (0, 0)]
    padded = jnp.pad(values, widths)
    total = jnp.zeros_like(values)
    for first in range(7):
        for second in range(7):
            total = total + padded[..., first:first + rows, second:second + cols, :] * kernel[first, second]
    center = lax.optimization_barrier(jnp.mean(total, axis=-1, keepdims=True))
    spread = lax.optimization_barrier(jnp.mean((total - center) ** 2, axis=-1, keepdims=True))
    return (total - center) * lax.rsqrt(spread + 1e-06) * gain

def rounded(values):
    return lax.optimization_barrier(values.astype(jnp.bfloat16)).astype(jnp.float32)

def reference(images, token_grads, counts, dw_kernel, ln_gain, w_in, w_out, layer_scale):
    channels = images.shape[-1]
    hidden_all = w_in.shape[-1]
    group = hidden_all // N_MP
    live = (jnp.arange(IMGS)[None, :] < counts[:, None]).astype(jnp.bfloat16)[:, :, None, None, None]
    inputs = (images * live).reshape((N_DP, MICRO) + images.shape[1:])
    upstream_all = (token_grads * live).reshape((N_DP, MICRO) + images.shape[1:])
    shape = (N_DP,) + images.shape[1:]
    grads_in = [jnp.zeros((N_DP, channels, hidden_all), jnp.float32) for s in range(SECTIONS)]
    grads_out = [jnp.zeros((N_DP, channels, hidden_all), jnp.float32) for s in range(SECTIONS)]
    for micro in range(MICRO):
        state = inputs[:, micro]
        stored = []
        for s in range(SECTIONS):
            stored.append(state)
            normed = mix_in(state, dw_kernel[s], ln_gain[s]).astype(jnp.bfloat16).reshape(-1, channels)
            hidden = jax.nn.gelu(jnp.dot(normed, w_in[s], preferred_element_type=jnp.float32), approximate=False).astype(jnp.bfloat16)
            parts = jnp.einsum('tkf,kfc->tkc', hidden.reshape(-1, N_MP, group).astype(jnp.float32), w_out[s].reshape(N_MP, group, channels).astype(jnp.float32))
            mixed = lax.optimization_barrier(jnp.sum(rounded(parts), axis=1))
            state = (state.astype(jnp.float32) + layer_scale[s] * mixed.reshape(shape)).astype(jnp.bfloat16)
        upstream = upstream_all[:, micro]
        for s in reversed(range(SECTIONS)):
            block_in = stored[s]
            normed32, pull = jax.vjp(lambda v: mix_in(v, dw_kernel[s], ln_gain[s]), block_in.astype(jnp.float32))
            normed = normed32.astype(jnp.bfloat16).reshape(-1, channels)
            before = jnp.dot(normed, w_in[s], preferred_element_type=jnp.float32)
            hidden = jax.nn.gelu(before, approximate=False).astype(jnp.bfloat16)
            branch = (upstream.astype(jnp.float32) * layer_scale[s]).astype(jnp.bfloat16).reshape(-1, channels)
            grads_out[s] = grads_out[s] + jnp.einsum('gtc,gtf->gcf', branch.reshape(N_DP, -1, channels).astype(jnp.float32), hidden.reshape(N_DP, -1, hidden_all).astype(jnp.float32))
            back_hidden = jnp.einsum('tc,fc->tf', branch.astype(jnp.float32), w_out[s].astype(jnp.float32))
            gelu_out, gelu_pull = jax.vjp(lambda v: jax.nn.gelu(v, approximate=False), before)
            back = gelu_pull(back_hidden)[0].astype(jnp.bfloat16)
            grads_in[s] = grads_in[s] + jnp.einsum('gtc,gtf->gcf', normed.reshape(N_DP, -1, channels).astype(jnp.float32), back.reshape(N_DP, -1, hidden_all).astype(jnp.float32))
            parts = jnp.einsum('tkf,ckf->tkc', back.reshape(-1, N_MP, group).astype(jnp.float32), w_in[s].reshape(channels, N_MP, group).astype(jnp.float32))
            dnorm = lax.optimization_barrier(jnp.sum(rounded(parts), axis=1))
            back_input = pull(dnorm.reshape(shape))[0]
            upstream = (upstream.astype(jnp.float32) + back_input).astype(jnp.bfloat16)
    grad_in = jnp.stack([lax.optimization_barrier(jnp.sum(rounded(grads_in[s]), axis=0)) for s in range(SECTIONS)]).astype(jnp.bfloat16)
    grad_out_t = jnp.stack([lax.optimization_barrier(jnp.sum(rounded(grads_out[s]), axis=0)) for s in range(SECTIONS)]).astype(jnp.bfloat16)
    return (grad_in, grad_out_t)
```

```python
import functools

import jax
import jax.numpy as jnp
from jax import lax
from jax.experimental import pallas as pl
from jax.experimental.pallas import tpu as pltpu
from jax.sharding import PartitionSpec as P

F32 = jnp.float32
BF16 = jnp.bfloat16

MP = 8
CHIPS = 4
DP = 16
SIDE = 4
DEPTH = 4
ROWS, COLS, TAPS = 8, 12, 7
TOK = ROWS * COLS
HALF = TOK // 2
C = 768
HALF_C = C // 2
HID = 384
LANES = 128
TAP_ROWS = TAPS * TAPS
GAIN, SCALE, INVERSE, PARAM_ROWS = TAP_ROWS, TAP_ROWS + 1, TAP_ROWS + 2, 56
OUT_ROWS = C // DP
PARAMS = pltpu.CompilerParams(vmem_limit_bytes=56 * 1024 * 1024)


def dot(a, b, contract=((1,), (0,))):
    return lax.dot_general(a, b, (contract, ((), ())), preferred_element_type=F32)


def depthwise(values, kernel_ref, lanes, flip):
    values = values.reshape(COLS, ROWS, LANES)
    row = lax.broadcasted_iota(jnp.int32, (COLS, ROWS, LANES), 1)
    edge = jnp.zeros((3, ROWS, LANES), F32)
    total = jnp.zeros((COLS, ROWS, LANES), F32)
    for a in range(TAPS):
        by = a - 3
        moved = values
        if by != 0:
            moved = pltpu.roll(moved, (-by) % ROWS, 1)
            moved = jnp.where((row + by >= 0) & (row + by < ROWS), moved, 0.0)
        wide = jnp.concatenate([edge, moved, edge], axis=0)
        for e in range(TAPS):
            at = a * TAPS + e
            if flip:
                at = TAPS * TAPS - 1 - at
            total = total + wide[e : e + COLS] * kernel_ref[at : at + 1, lanes][None]
    return total.reshape(TOK, LANES)


def each_lanes(body):
    @pl.loop(0, C // LANES)
    def _(tile):
        body(pl.ds(pl.multiple_of(tile * LANES, LANES), LANES))


def gelu_parts(before):
    half = 0.5 * (1.0 + lax.erf(before * (0.5**0.5)))
    density = jnp.exp(-0.5 * before * before) * 0.3989422804014327
    return (before * half).astype(BF16), half + before * density


class Weights:
    AHEAD = 3

    def __init__(self, refs, places, buffer, sems, slope=None, slopes=None):
        self.places = places
        self.copies = []
        for at, (ref, group) in enumerate(zip(refs, places)):
            copies = [pltpu.make_async_copy(ref, buffer.at[group], sems.at[at])]
            if slope is not None:
                copies.append(
                    pltpu.make_async_copy(
                        slope.at[group], slopes.at[group], sems.at[MP + group]
                    )
                )
            self.copies.append(copies)
        for at in range(min(self.AHEAD, len(places))):
            self.start(at)

    def start(self, at):
        for copy in self.copies[at]:
            copy.start()

    def __iter__(self):
        for at, group in enumerate(self.places):
            for copy in self.copies[at]:
                copy.wait()
            if at + self.AHEAD < len(self.places):
                self.start(at + self.AHEAD)
            yield group


class Moves:
    def __init__(self, sems, base):
        self.sems, self.at, self.copies = sems, base, []

    def start(self, source, target):
        copy = pltpu.make_async_copy(source, target, self.sems.at[self.at])
        self.at += 1
        copy.start()
        self.copies.append(copy)

    def wait(self):
        for copy in self.copies:
            copy.wait()
        self.copies = []


def normalise(x, params, conv, normed_out):
    def convolve(lanes):
        conv[:, lanes] = depthwise(x[:, lanes].astype(F32), params, lanes, False)

    each_lanes(convolve)
    values = conv[...]
    mean = jnp.sum(values, axis=1, keepdims=True) * (1.0 / C)
    centered = values - mean
    var = jnp.sum(centered * centered, axis=1, keepdims=True) * (1.0 / C)
    rstd = lax.rsqrt(var + 1e-6)
    normed_out[...] = (centered * rstd * params[GAIN : GAIN + 1]).astype(BF16)
    return rstd


def expand(normed, buffer, group):
    before = dot(normed[:, :HALF_C], buffer[group, :HID, :HID])
    return before + dot(normed[:, HALF_C:], buffer[group, :HID, HID:])


WIDE = jax.ShapeDtypeStruct((TOK, C), BF16)
SUMS = jax.ShapeDtypeStruct((TOK, C), F32)
RSTD = jax.ShapeDtypeStruct((TOK, LANES), F32)
SLOPE = jax.ShapeDtypeStruct((MP, TOK, HID), F32)
SCRATCH = {
    "tokens": pltpu.VMEM((TOK, C), BF16),
    "grads": pltpu.VMEM((TOK, C), BF16),
    "branch": pltpu.VMEM((TOK, C), BF16),
    "normed_here": pltpu.VMEM((TOK, C), BF16),
    "params_here": pltpu.VMEM((PARAM_ROWS, C), F32),
    "rstd_here": pltpu.VMEM((TOK, LANES), F32),
    "total": pltpu.VMEM((TOK, C), F32),
    "slopes": pltpu.VMEM((MP, TOK, HID), F32),
    "buffer": pltpu.VMEM((MP, C, C), BF16),
    "sems": pltpu.SemaphoreType.DMA((40,)),
}


def forward_body(r, weights, places):
    loads, saves = Moves(r["sems"], 2 * MP), Moves(r["sems"], 2 * MP + 8)
    total, normed, params = r["total"], r["normed_here"], r["params_here"]
    first, save = "x" in r, "slope" in r
    if first:
        loads.start(r["x"], r["tokens"])
        loads.start(r["params"], params)
    else:
        loads.start(r["normed_in"], normed)
        loads.start(r["sums_in"], total)
    groups = Weights(weights, places, r["buffer"], r["sems"])
    loads.wait()
    if first:
        rstd = normalise(r["tokens"], params, total, normed)
        saves.start(normed, r["normed"])
        total[...] = jnp.zeros((TOK, C), F32)
    if save:
        r["rstd_here"][...] = jnp.broadcast_to(rstd, (TOK, LANES))
        saves.start(r["rstd_here"], r["rstd"])
    for group in groups:
        hidden, slope = gelu_parts(expand(normed, r["buffer"], group))
        if save:
            r["slopes"][group] = slope
            saves.start(r["slopes"].at[group], r["slope"].at[group])
        part = dot(hidden, r["buffer"][group, HID:, :])
        total[...] += part.astype(BF16).astype(F32)
    if "out" in r:
        x = r["tokens"][...].astype(F32)
        scale = params[SCALE : SCALE + 1]
        r["branch"][...] = (x + scale * total[...]).astype(BF16)
        saves.start(r["branch"], r["out"])
    else:
        saves.start(total, r["sums"])
    saves.wait()


def pull_back(r, groups, rstd):
    g, params, total, branch = r["grads"], r["params_here"], r["total"], r["branch"]
    branch[...] = (g[...].astype(F32) * params[SCALE : SCALE + 1]).astype(BF16)
    total[...] = jnp.zeros((TOK, C), F32)
    for group in groups:
        spread = dot(branch[...], r["buffer"][group, HID:, :], ((1,), (1,)))
        back = (spread * r["slopes"][group]).astype(BF16)
        for half in range(2):
            lanes = slice(half * HALF_C, (half + 1) * HALF_C)
            part = dot(back, r["buffer"][group, :HID, lanes], ((1,), (1,)))
            total[:, lanes] += part.astype(BF16).astype(F32)
    inner = total[...] * params[GAIN : GAIN + 1]
    xhat = r["normed_here"][...].astype(F32) * params[INVERSE : INVERSE + 1]
    first = jnp.sum(inner, axis=1, keepdims=True) * (1.0 / C)
    second = jnp.sum(inner * xhat, axis=1, keepdims=True) * (1.0 / C)
    total[...] = (inner - first - xhat * second) * rstd

    def convolve(lanes):
        value = depthwise(total[:, lanes], params, lanes, True)
        branch[:, lanes] = (g[:, lanes].astype(F32) + value).astype(BF16)

    each_lanes(convolve)


def backward_body(r, weights, places):
    loads, saves = Moves(r["sems"], 2 * MP), Moves(r["sems"], 2 * MP + 8)
    loads.start(r["g"], r["grads"])
    loads.start(r["params"], r["params_here"])
    loads.start(r["normed_in"], r["normed_here"])
    loads.start(r["rstd_in"], r["rstd_here"])
    groups = Weights(
        weights, places, r["buffer"], r["sems"], r["slope_in"], r["slopes"]
    )
    loads.wait()
    pull_back(r, groups, r["rstd_here"][:, :1])
    saves.start(r["branch"], r["out"])
    saves.wait()


def turn_body(r, weights, places):
    loads, saves = Moves(r["sems"], 2 * MP), Moves(r["sems"], 2 * MP + 8)
    loads.start(r["x"], r["tokens"])
    loads.start(r["params"], r["params_here"])
    loads.start(r["g"], r["grads"])
    groups = Weights(weights, places, r["buffer"], r["sems"])
    loads.wait()
    rstd = normalise(r["tokens"], r["params_here"], r["total"], r["normed_here"])
    saves.start(r["normed_here"], r["normed"])
    for group in groups:
        r["slopes"][group] = gelu_parts(expand(r["normed_here"], r["buffer"], group))[1]
    pull_back(r, range(MP), rstd)
    saves.start(r["branch"], r["out"])
    saves.wait()


def block_kernel(body, names, places, sc, *refs):
    r = dict(zip(names, refs))

    @pl.when(sc[0] == 1)
    def _():
        body(r, [r[at] for at in range(len(places))], places)


def call_block(body, active, operands, weights, places, outs):
    anywhere = pl.BlockSpec(memory_space=pl.ANY)
    pieces = len(weights)
    names = list(operands) + list(range(pieces)) + list(outs) + list(SCRATCH)
    results = pl.pallas_call(
        functools.partial(block_kernel, body, names, places),
        in_specs=[pl.BlockSpec(memory_space=pltpu.SMEM)]
        + [anywhere] * (len(operands) + pieces),
        out_specs=[anywhere] * len(outs),
        out_shape=list(outs.values()),
        scratch_shapes=list(SCRATCH.values()),
        cost_estimate=pl.CostEstimate(
            flops=4 * TOK * C * HID * pieces,
            bytes_accessed=2 * C * C * pieces,
            transcendentals=0,
        ),
        compiler_params=PARAMS,
    )(active, *operands.values(), *weights)
    return dict(zip(outs, results))


def grads_kernel(sc, recv, scale, w_in, w_out, keep, give):
    place = sc[0]
    normed = jnp.concatenate([recv[k, :HALF] for k in range(MP)], axis=0)
    g = jnp.concatenate([recv[k, HALF:] for k in range(MP)], axis=0)
    branch = (g.astype(F32) * scale[...]).astype(BF16)
    hidden, slope = gelu_parts(dot(normed, w_in[...]))
    back = (dot(branch, w_out[...], ((1,), (1,))) * slope).astype(BF16)
    for half in range(2):
        lanes = slice(half * HALF_C, (half + 1) * HALF_C)
        gin = dot(normed[:, lanes], back, ((0,), (0,))).astype(BF16)
        gout = dot(branch[:, lanes], hidden, ((0,), (0,))).astype(BF16)
        for part in range(DP // 2):
            rows = slice(part * OUT_ROWS, (part + 1) * OUT_ROWS)
            block = jnp.concatenate([gin[rows], gout[rows]], axis=1)
            owner = half * (DP // 2) + part
            low, high = owner % 2, owner % SIDE // 2
            slot = jnp.where(high == place // 2, 0, SIDE) + owner // SIDE

            @pl.when(low == lax.rem(place, 2))
            def _():
                keep[slot] = block

            @pl.when(low != lax.rem(place, 2))
            def _():
                give[slot] = block


def run_grads(sc, recv, scale, w_in, w_out):
    vmem = pl.BlockSpec(memory_space=pltpu.VMEM)
    eight = jax.ShapeDtypeStruct((DP // 2, OUT_ROWS, 2 * HID), BF16)
    return pl.pallas_call(
        grads_kernel,
        in_specs=[pl.BlockSpec(memory_space=pltpu.SMEM)] + [vmem] * 4,
        out_specs=[vmem] * 2,
        out_shape=[eight, eight],
        compiler_params=PARAMS,
    )(sc, recv, scale, w_in, w_out)


def sum_over_dp(keep, give):
    add = lambda a, b: (a.astype(F32) + b.astype(F32)).astype(BF16)
    trade = lambda v, by: lax.ppermute(v, "dp", [(z, z ^ by) for z in range(DP)])
    value = add(keep, trade(give, 1))
    value = add(value[:SIDE], trade(value[SIDE:], 2))
    groups = [[low + SIDE * k for k in range(SIDE)] for low in range(SIDE)]
    value = lax.all_to_all(value, "dp", 0, 0, axis_index_groups=groups, tiled=True)
    total = jnp.sum(value.astype(F32), axis=0)
    return total.astype(BF16)


def shards(images, token_grads, counts, dw_kernel, ln_gain, w_in, w_out, layer_scale):
    s = lax.axis_index("section")
    j = lax.axis_index("mp")
    chip, core = j // 2, j % 2
    w_in, w_out = w_in[0], w_out[0]

    up = [(i, (i + 2) % MP) for i in range(MP)]
    down = [(i, (i - 2) % MP) for i in range(MP)]
    swap = [(i, i ^ 1) for i in range(MP)]
    move = lambda v, pairs: lax.ppermute(v, "mp", pairs)
    own = jnp.concatenate(
        [jnp.concatenate([w_in[:HALF_C], w_in[HALF_C:]], axis=1), w_out], axis=0
    )
    sample, image = chip // 2, chip % 2
    live = (image < lax.dynamic_index_in_dim(counts, sample, 0, keepdims=False)).astype(BF16)
    one = lambda v: (
        lax.dynamic_index_in_dim(
            v.reshape((CHIPS,) + v.shape[2:]), chip, 0, keepdims=False
        )
        * live
    ).transpose(1, 0, 2).reshape(TOK, C)

    x, g = one(images), one(token_grads)
    params = jnp.concatenate(
        [
            dw_kernel.reshape(TAP_ROWS, C),
            ln_gain,
            layer_scale,
            1.0 / ln_gain,
            jnp.zeros((PARAM_ROWS - TAP_ROWS - 3, C), F32),
        ]
    )
    around = [(i, (i + 2 - 4 * (i % 2)) % MP) for i in range(MP)]
    counter = [(i, (i - 2 + 4 * (i % 2)) % MP) for i in range(MP)]
    first = move(own, around)
    first, own, x, g, params = lax.optimization_barrier((first, own, x, g, params))
    second = move(own, counter)
    third = move(first, around)

    active = [(s == block).astype(jnp.int32)[None] for block in range(DEPTH)]
    send = lambda v, source, to: lax.ppermute(v, "section", [(source, to)])

    result = call_block(
        forward_body,
        active[0],
        dict(x=x, params=params),
        [own, first],
        [0, 1],
        dict(normed=WIDE, sums=SUMS),
    )
    normed = result["normed"]
    swap_own, swap_first, sums = lax.optimization_barrier((own, first, result["sums"]))
    result = call_block(
        forward_body,
        active[0],
        dict(normed_in=normed, sums_in=sums),
        [second, third],
        [0, 1],
        dict(sums=SUMS),
    )
    mixed = result["sums"].astype(BF16)
    mixed = mixed.astype(F32) + move(mixed, swap).astype(F32)
    out = (x.astype(F32) + layer_scale * mixed).astype(BF16)

    weights = [own, first, move(swap_own, swap), move(swap_first, swap)]
    weights += [second, third, move(second, swap), move(third, swap)]
    places = list(range(MP))
    normed_of, saved = [normed], [None]
    for block in range(1, DEPTH - 1):
        result = call_block(
            forward_body,
            active[block],
            dict(x=send(out, block - 1, block), params=params),
            weights,
            places,
            dict(out=WIDE, normed=WIDE, rstd=RSTD, slope=SLOPE),
        )
        out = result["out"]
        normed_of.append(result["normed"])
        saved.append(result)
    result = call_block(
        turn_body,
        active[DEPTH - 1],
        dict(x=send(out, DEPTH - 2, DEPTH - 1), g=g, params=params),
        weights,
        places,
        dict(out=WIDE, normed=WIDE),
    )
    normed_of.append(result["normed"])
    g_of = [g]
    for block in range(DEPTH - 2, 0, -1):
        g = send(result["out"], block + 1, block)
        g_of.append(g)
        kept = saved[block]
        result = call_block(
            backward_body,
            active[block],
            dict(
                g=g,
                params=params,
                normed_in=kept["normed"],
                rstd_in=kept["rstd"],
                slope_in=kept["slope"],
            ),
            weights,
            places,
            dict(out=WIDE),
        )
    g_of.append(send(result["out"], 1, 0))

    pick = lambda values: lax.select_n(s, *values)
    mine = jnp.stack([pick(normed_of), pick(g_of[::-1])])
    mine = jnp.where(core == 0, mine[:, :HALF], mine[:, HALF:]).reshape(TOK, C)
    recv = lax.all_to_all(
        jnp.broadcast_to(mine[None], (MP, TOK, C)), "mp", 0, 0, tiled=True
    )
    z = lax.axis_index("dp")
    place = (z % SIDE).astype(jnp.int32)[None]
    total = sum_over_dp(*run_grads(place, recv, layer_scale, w_in, w_out))
    return total[None, :, :HID], total[None, :, HID:]


def solution(mesh):
    return jax.shard_map(
        shards,
        mesh=mesh,
        in_specs=(
            P("dp", None, None, None, None),
            P("dp", None, None, None, None),
            P("dp"),
            P("section", None, None, None),
            P("section", None),
            P("section", None, "mp"),
            P("section", "mp", None),
            P("section", None),
        ),
        out_specs=(P("section", "dp", "mp"), P("section", "dp", "mp")),
        check_vma=False,
    )
```

```python
import functools

import jax
import jax.numpy as jnp
from jax import lax
from jax.experimental import pallas as pl
from jax.experimental.pallas import tpu as pltpu
from jax.sharding import PartitionSpec as P

F32 = jnp.float32
BF16 = jnp.bfloat16

MP = 8
CHIPS = 4
DP = 16
SIDE = 4
DEPTH = 4
ROWS, COLS, TAPS = 8, 12, 7
TOK = ROWS * COLS
HALF = TOK // 2
C = 768
HALF_C = C // 2
HID = 384
LANES = 128
TAP_ROWS = TAPS * TAPS
GAIN, SCALE, INVERSE, PARAM_ROWS = TAP_ROWS, TAP_ROWS + 1, TAP_ROWS + 2, 56
OUT_ROWS = C // DP
PARAMS = pltpu.CompilerParams(vmem_limit_bytes=56 * 1024 * 1024)
SMALL = pltpu.CompilerParams(vmem_limit_bytes=24 * 1024 * 1024)


def dot(a, b, contract=((1,), (0,))):
    return lax.dot_general(a, b, (contract, ((), ())), preferred_element_type=F32)


def depthwise(values, kernel_ref, lanes, flip):
    values = values.reshape(COLS, ROWS, LANES)
    row = lax.broadcasted_iota(jnp.int32, (COLS, ROWS, LANES), 1)
    edge = jnp.zeros((3, ROWS, LANES), F32)
    total = jnp.zeros((COLS, ROWS, LANES), F32)
    for a in range(TAPS):
        by = a - 3
        moved = values
        if by != 0:
            moved = pltpu.roll(moved, (-by) % ROWS, 1)
            moved = jnp.where((row + by >= 0) & (row + by < ROWS), moved, 0.0)
        wide = jnp.concatenate([edge, moved, edge], axis=0)
        for e in range(TAPS):
            at = a * TAPS + e
            if flip:
                at = TAPS * TAPS - 1 - at
            total = total + wide[e : e + COLS] * kernel_ref[at : at + 1, lanes][None]
    return total.reshape(TOK, LANES)


def each_lanes(body):
    @pl.loop(0, C // LANES)
    def _(tile):
        body(pl.ds(pl.multiple_of(tile * LANES, LANES), LANES))


def gelu_parts(before):
    half = 0.5 * (1.0 + lax.erf(before * (0.5**0.5)))
    density = jnp.exp(-0.5 * before * before) * 0.3989422804014327
    return (before * half).astype(BF16), half + before * density


class Weights:
    AHEAD = 3

    def __init__(self, refs, places, buffer, sems, slope=None, slopes=None):
        self.places = places
        self.copies = []
        for at, (ref, group) in enumerate(zip(refs, places)):
            copies = [pltpu.make_async_copy(ref, buffer.at[group], sems.at[at])]
            if slope is not None:
                copies.append(
                    pltpu.make_async_copy(
                        slope.at[group], slopes.at[group], sems.at[MP + group]
                    )
                )
            self.copies.append(copies)
        for at in range(min(self.AHEAD, len(places))):
            self.start(at)

    def start(self, at):
        for copy in self.copies[at]:
            copy.start()

    def __iter__(self):
        for at, group in enumerate(self.places):
            for copy in self.copies[at]:
                copy.wait()
            if at + self.AHEAD < len(self.places):
                self.start(at + self.AHEAD)
            yield group


class Moves:
    def __init__(self, sems, base):
        self.sems, self.at, self.copies = sems, base, []

    def start(self, source, target):
        copy = pltpu.make_async_copy(source, target, self.sems.at[self.at])
        self.at += 1
        copy.start()
        self.copies.append(copy)

    def wait(self):
        for copy in self.copies:
            copy.wait()
        self.copies = []


def normalise(x, params, conv, normed_out):
    def convolve(lanes):
        conv[:, lanes] = depthwise(x[:, lanes].astype(F32), params, lanes, False)

    each_lanes(convolve)
    values = conv[...]
    mean = jnp.sum(values, axis=1, keepdims=True) * (1.0 / C)
    centered = values - mean
    var = jnp.sum(centered * centered, axis=1, keepdims=True) * (1.0 / C)
    rstd = lax.rsqrt(var + 1e-6)
    normed_out[...] = (centered * rstd * params[GAIN : GAIN + 1]).astype(BF16)
    return rstd


def expand(normed, buffer, group):
    before = dot(normed[:, :HALF_C], buffer[group, :HID, :HID])
    return before + dot(normed[:, HALF_C:], buffer[group, :HID, HID:])


WIDE = jax.ShapeDtypeStruct((TOK, C), BF16)
SUMS = jax.ShapeDtypeStruct((TOK, C), F32)
RSTD = jax.ShapeDtypeStruct((TOK, LANES), F32)
SLOPE = jax.ShapeDtypeStruct((MP, TOK, HID), F32)
SCRATCH = {
    "tokens": pltpu.VMEM((TOK, C), BF16),
    "grads": pltpu.VMEM((TOK, C), BF16),
    "branch": pltpu.VMEM((TOK, C), BF16),
    "normed_here": pltpu.VMEM((TOK, C), BF16),
    "params_here": pltpu.VMEM((PARAM_ROWS, C), F32),
    "rstd_here": pltpu.VMEM((TOK, LANES), F32),
    "total": pltpu.VMEM((TOK, C), F32),
    "slopes": pltpu.VMEM((MP, TOK, HID), F32),
    "buffer": pltpu.VMEM((MP, C, C), BF16),
    "sems": pltpu.SemaphoreType.DMA((40,)),
}


def forward_body(r, weights, places):
    loads, saves = Moves(r["sems"], 2 * MP), Moves(r["sems"], 2 * MP + 8)
    total, normed, params = r["total"], r["normed_here"], r["params_here"]
    first, save = "x" in r, "slope" in r
    if first:
        loads.start(r["x"], r["tokens"])
        loads.start(r["params"], params)
    else:
        loads.start(r["normed_in"], normed)
        loads.start(r["sums_in"], total)
    groups = Weights(weights, places, r["buffer"], r["sems"])
    loads.wait()
    if first:
        rstd = normalise(r["tokens"], params, total, normed)
        saves.start(normed, r["normed"])
        total[...] = jnp.zeros((TOK, C), F32)
    if save:
        r["rstd_here"][...] = jnp.broadcast_to(rstd, (TOK, LANES))
        saves.start(r["rstd_here"], r["rstd"])
    for group in groups:
        hidden, slope = gelu_parts(expand(normed, r["buffer"], group))
        if save:
            r["slopes"][group] = slope
            saves.start(r["slopes"].at[group], r["slope"].at[group])
        part = dot(hidden, r["buffer"][group, HID:, :])
        total[...] += part.astype(BF16).astype(F32)
    if "out" in r:
        x = r["tokens"][...].astype(F32)
        scale = params[SCALE : SCALE + 1]
        r["branch"][...] = (x + scale * total[...]).astype(BF16)
        saves.start(r["branch"], r["out"])
    elif "part" in r:
        r["branch"][...] = total[...].astype(BF16)
        saves.start(r["branch"], r["part"])
    else:
        saves.start(total, r["sums"])
    saves.wait()


def join_body(r, weights, places):
    loads, saves = Moves(r["sems"], 2 * MP), Moves(r["sems"], 2 * MP + 8)
    loads.start(r["x"], r["tokens"])
    loads.start(r["params"], r["params_here"])
    loads.start(r["mine"], r["grads"])
    loads.start(r["other"], r["normed_here"])
    loads.wait()
    mixed = r["grads"][...].astype(F32) + r["normed_here"][...].astype(F32)
    x = r["tokens"][...].astype(F32)
    scale = r["params_here"][SCALE : SCALE + 1]
    r["branch"][...] = (x + scale * mixed).astype(BF16)
    saves.start(r["branch"], r["out"])
    saves.wait()


def pull_back(r, groups, rstd):
    g, params, total, branch = r["grads"], r["params_here"], r["total"], r["branch"]
    branch[...] = (g[...].astype(F32) * params[SCALE : SCALE + 1]).astype(BF16)
    total[...] = jnp.zeros((TOK, C), F32)
    for group in groups:
        spread = dot(branch[...], r["buffer"][group, HID:, :], ((1,), (1,)))
        back = (spread * r["slopes"][group]).astype(BF16)
        for half in range(2):
            lanes = slice(half * HALF_C, (half + 1) * HALF_C)
            part = dot(back, r["buffer"][group, :HID, lanes], ((1,), (1,)))
            total[:, lanes] += part.astype(BF16).astype(F32)
    inner = total[...] * params[GAIN : GAIN + 1]
    xhat = r["normed_here"][...].astype(F32) * params[INVERSE : INVERSE + 1]
    first = jnp.sum(inner, axis=1, keepdims=True) * (1.0 / C)
    second = jnp.sum(inner * xhat, axis=1, keepdims=True) * (1.0 / C)
    total[...] = (inner - first - xhat * second) * rstd

    def convolve(lanes):
        value = depthwise(total[:, lanes], params, lanes, True)
        branch[:, lanes] = (g[:, lanes].astype(F32) + value).astype(BF16)

    each_lanes(convolve)


def backward_body(r, weights, places):
    loads, saves = Moves(r["sems"], 2 * MP), Moves(r["sems"], 2 * MP + 8)
    loads.start(r["g"], r["grads"])
    loads.start(r["params"], r["params_here"])
    loads.start(r["normed_in"], r["normed_here"])
    loads.start(r["rstd_in"], r["rstd_here"])
    groups = Weights(
        weights, places, r["buffer"], r["sems"], r["slope_in"], r["slopes"]
    )
    loads.wait()
    pull_back(r, groups, r["rstd_here"][:, :1])
    saves.start(r["branch"], r["out"])
    saves.wait()


def turn_body(r, weights, places):
    loads, saves = Moves(r["sems"], 2 * MP), Moves(r["sems"], 2 * MP + 8)
    loads.start(r["x"], r["tokens"])
    loads.start(r["params"], r["params_here"])
    loads.start(r["g"], r["grads"])
    groups = Weights(weights, places, r["buffer"], r["sems"])
    loads.wait()
    rstd = normalise(r["tokens"], r["params_here"], r["total"], r["normed_here"])
    saves.start(r["normed_here"], r["normed"])
    for group in groups:
        r["slopes"][group] = gelu_parts(expand(r["normed_here"], r["buffer"], group))[1]
    pull_back(r, range(MP), rstd)
    saves.start(r["branch"], r["out"])
    saves.wait()


def block_kernel(body, names, places, sc, *refs):
    r = dict(zip(names, refs))

    @pl.when(sc[0] == 1)
    def _():
        body(r, [r[at] for at in range(len(places))], places)


def call_block(body, active, operands, weights, places, outs):
    anywhere = pl.BlockSpec(memory_space=pl.ANY)
    pieces = len(weights)
    names = list(operands) + list(range(pieces)) + list(outs) + list(SCRATCH)
    results = pl.pallas_call(
        functools.partial(block_kernel, body, names, places),
        in_specs=[pl.BlockSpec(memory_space=pltpu.SMEM)]
        + [anywhere] * (len(operands) + pieces),
        out_specs=[anywhere] * len(outs),
        out_shape=list(outs.values()),
        scratch_shapes=list(SCRATCH.values()),
        cost_estimate=pl.CostEstimate(
            flops=4 * TOK * C * HID * max(pieces, 1),
            bytes_accessed=2 * C * C * max(pieces, 1),
            transcendentals=0,
        ),
        compiler_params=PARAMS,
    )(active, *operands.values(), *weights)
    return dict(zip(outs, results))


def grads_kernel(sc, recv, other, scale, w_in, w_out, keep, give):
    early_here, late_here, core = sc[0], sc[1], sc[2]
    shares = [ref[k] for ref in (recv, other) for k in range(CHIPS)]
    normed = jnp.concatenate([share[:HALF] for share in shares], axis=0)
    g = jnp.concatenate([share[HALF:] for share in shares], axis=0)
    branch = (g.astype(F32) * scale[...]).astype(BF16)
    hidden, slope = gelu_parts(dot(normed, w_in[...]))
    back = (dot(branch, w_out[...], ((1,), (1,))) * slope).astype(BF16)
    for half in range(2):
        lanes = slice(half * HALF_C, (half + 1) * HALF_C)
        gin = dot(normed[:, lanes], back, ((0,), (0,))).astype(BF16)
        gout = dot(branch[:, lanes], hidden, ((0,), (0,))).astype(BF16)
        for part in range(DP // 2):
            rows = slice(part * OUT_ROWS, (part + 1) * OUT_ROWS)
            block = jnp.concatenate([gin[rows], gout[rows]], axis=1)
            owner = half * (DP // 2) + part
            low, high = owner % 2, owner % SIDE // 2
            early = jnp.where(core == 0, low, high)
            late = jnp.where(core == 0, high, low)
            slot = jnp.where(late == late_here, 0, SIDE) + owner // SIDE

            @pl.when(early == early_here)
            def _():
                keep[slot] = block

            @pl.when(early != early_here)
            def _():
                give[slot] = block


def run_grads(sc, recv, other, scale, w_in, w_out):
    vmem = pl.BlockSpec(memory_space=pltpu.VMEM)
    eight = jax.ShapeDtypeStruct((DP // 2, OUT_ROWS, 2 * HID), BF16)
    return pl.pallas_call(
        grads_kernel,
        in_specs=[pl.BlockSpec(memory_space=pltpu.SMEM)] + [vmem] * 5,
        out_specs=[vmem] * 2,
        out_shape=[eight, eight],
        compiler_params=SMALL,
    )(sc, recv, other, scale, w_in, w_out)


def sum_over_dp(keep, give):
    add = lambda a, b: (a.astype(F32) + b.astype(F32)).astype(BF16)
    trade = lambda v, by: lax.ppermute(
        v,
        ("dp", "mp"),
        [(z * MP + j, (z ^ by[j % 2]) * MP + j) for z in range(DP) for j in range(MP)],
    )
    value = add(keep, trade(give, (1, 2)))
    value = add(value[:SIDE], trade(value[SIDE:], (2, 1)))
    here = lax.axis_index("dp") // SIDE
    block = lambda ahead: lax.dynamic_index_in_dim(
        value, (here + ahead) % SIDE, 0, keepdims=False
    )
    total = block(0).astype(F32)
    for ahead in range(1, SIDE):
        pairs = [(z, (z + ahead * SIDE) % DP) for z in range(DP)]
        total = total + lax.ppermute(block(ahead), "dp", pairs).astype(F32)
    return total.astype(BF16)


def shards(images, token_grads, counts, dw_kernel, ln_gain, w_in, w_out, layer_scale):
    s = lax.axis_index("section")
    j = lax.axis_index("mp")
    chip, core = j // 2, j % 2
    w_in, w_out = w_in[0], w_out[0]

    up = [(i, (i + 2) % MP) for i in range(MP)]
    down = [(i, (i - 2) % MP) for i in range(MP)]
    swap = [(i, i ^ 1) for i in range(MP)]
    move = lambda v, pairs: lax.ppermute(v, "mp", pairs)
    own = jnp.concatenate(
        [jnp.concatenate([w_in[:HALF_C], w_in[HALF_C:]], axis=1), w_out], axis=0
    )
    sample, image = chip // 2, chip % 2
    live = (image < lax.dynamic_index_in_dim(counts, sample, 0, keepdims=False)).astype(BF16)
    one = lambda v: (
        lax.dynamic_index_in_dim(
            v.reshape((CHIPS,) + v.shape[2:]), chip, 0, keepdims=False
        )
        * live
    ).transpose(1, 0, 2).reshape(TOK, C)

    x, g = one(images), one(token_grads)
    params = jnp.concatenate(
        [
            dw_kernel.reshape(TAP_ROWS, C),
            ln_gain,
            layer_scale,
            1.0 / ln_gain,
            jnp.zeros((PARAM_ROWS - TAP_ROWS - 3, C), F32),
        ]
    )
    around = [(i, (i + 2 - 4 * (i % 2)) % MP) for i in range(MP)]
    counter = [(i, (i - 2 + 4 * (i % 2)) % MP) for i in range(MP)]
    first = move(own, around)
    first, own, x, g, params = lax.optimization_barrier((first, own, x, g, params))
    second = move(own, counter)
    third = move(first, around)

    active = [(s == block).astype(jnp.int32)[None] for block in range(DEPTH)]
    send = lambda v, source, to: lax.ppermute(v, "section", [(source, to)])

    result = call_block(
        forward_body,
        active[0],
        dict(x=x, params=params),
        [own, first],
        [0, 1],
        dict(normed=WIDE, sums=SUMS),
    )
    normed = result["normed"]
    swap_own, swap_first, sums = lax.optimization_barrier((own, first, result["sums"]))
    result = call_block(
        forward_body,
        active[0],
        dict(normed_in=normed, sums_in=sums),
        [second, third],
        [0, 1],
        dict(part=WIDE),
    )
    swap_second, swap_third, part = lax.optimization_barrier((second, third, result["part"]))
    result = call_block(
        join_body,
        active[0],
        dict(x=x, params=params, mine=part, other=move(part, swap)),
        [],
        [],
        dict(out=WIDE),
    )
    out = result["out"]

    weights = [own, first, move(swap_own, swap), move(swap_first, swap)]
    weights += [second, third, move(swap_second, swap), move(swap_third, swap)]
    places = list(range(MP))
    normed_of, saved = [normed], [None]
    for block in range(1, DEPTH - 1):
        result = call_block(
            forward_body,
            active[block],
            dict(x=send(out, block - 1, block), params=params),
            weights,
            places,
            dict(out=WIDE, normed=WIDE, rstd=RSTD, slope=SLOPE),
        )
        out = result["out"]
        normed_of.append(result["normed"])
        saved.append(result)
    result = call_block(
        turn_body,
        active[DEPTH - 1],
        dict(x=send(out, DEPTH - 2, DEPTH - 1), g=g, params=params),
        weights,
        places,
        dict(out=WIDE, normed=WIDE),
    )
    normed_of.append(result["normed"])
    g_of = [g]
    for block in range(DEPTH - 2, 0, -1):
        g = send(result["out"], block + 1, block)
        g_of.append(g)
        kept = saved[block]
        result = call_block(
            backward_body,
            active[block],
            dict(
                g=g,
                params=params,
                normed_in=kept["normed"],
                rstd_in=kept["rstd"],
                slope_in=kept["slope"],
            ),
            weights,
            places,
            dict(out=WIDE),
        )
    g_of.append(send(result["out"], 1, 0))

    pick = lambda values: lax.select_n(s, *values)
    mine = jnp.stack([pick(normed_of), pick(g_of[::-1])])
    mine = jnp.where(core == 0, mine[:, :HALF], mine[:, HALF:]).reshape(TOK, C)
    recv = lax.all_to_all(
        jnp.broadcast_to(mine[None], (CHIPS, TOK, C)),
        "mp",
        0,
        0,
        axis_index_groups=[list(range(0, MP, 2)), list(range(1, MP, 2))],
        tiled=True,
    )
    other = move(recv, swap)
    z = lax.axis_index("dp")
    low, high = z % 2, z % SIDE // 2
    place = [jnp.where(core == 0, low, high), jnp.where(core == 0, high, low), core]
    place = jnp.stack([jnp.asarray(v, jnp.int32) for v in place])
    total = sum_over_dp(*run_grads(place, recv, other, layer_scale, w_in, w_out))
    return total[None, :, :HID], total[None, :, HID:]


def solution(mesh):
    return jax.shard_map(
        shards,
        mesh=mesh,
        in_specs=(
            P("dp", None, None, None, None),
            P("dp", None, None, None, None),
            P("dp"),
            P("section", None, None, None),
            P("section", None),
            P("section", None, "mp"),
            P("section", "mp", None),
            P("section", None),
        ),
        out_specs=(P("section", "dp", "mp"), P("section", "dp", "mp")),
        check_vma=False,
    )
```

```python
import functools

import jax
import jax.numpy as jnp
from jax import lax
from jax.experimental import pallas as pl
from jax.experimental.pallas import tpu as pltpu
from jax.sharding import PartitionSpec as P

F32 = jnp.float32
BF16 = jnp.bfloat16

MP = 8
CHIPS = 4
DP = 16
SIDE = 4
DEPTH = 4
ROWS, COLS, TAPS = 8, 12, 7
TOK = ROWS * COLS
HALF = TOK // 2
C = 768
HALF_C = C // 2
HID = 384
LANES = 128
TAP_ROWS = TAPS * TAPS
GAIN, SCALE, INVERSE, PARAM_ROWS = TAP_ROWS, TAP_ROWS + 1, TAP_ROWS + 2, 56
OUT_ROWS = C // DP
SMALL = pltpu.CompilerParams(vmem_limit_bytes=24 * 1024 * 1024)


def dot(a, b, contract=((1,), (0,))):
    return lax.dot_general(a, b, (contract, ((), ())), preferred_element_type=F32)


def depthwise(values, kernel_ref, lanes, flip):
    values = values.reshape(COLS, ROWS, LANES)
    row = lax.broadcasted_iota(jnp.int32, (COLS, ROWS, LANES), 1)
    edge = jnp.zeros((3, ROWS, LANES), F32)
    total = jnp.zeros((COLS, ROWS, LANES), F32)
    for a in range(TAPS):
        by = a - 3
        moved = values
        if by != 0:
            moved = pltpu.roll(moved, (-by) % ROWS, 1)
            moved = jnp.where((row + by >= 0) & (row + by < ROWS), moved, 0.0)
        wide = jnp.concatenate([edge, moved, edge], axis=0)
        for e in range(TAPS):
            at = a * TAPS + e
            if flip:
                at = TAPS * TAPS - 1 - at
            total = total + wide[e : e + COLS] * kernel_ref[at : at + 1, lanes][None]
    return total.reshape(TOK, LANES)


def each_lanes(body):
    @pl.loop(0, C // LANES)
    def _(tile):
        body(pl.ds(pl.multiple_of(tile * LANES, LANES), LANES))


def gelu_parts(before):
    half = 0.5 * (1.0 + lax.erf(before * (0.5**0.5)))
    density = jnp.exp(-0.5 * before * before) * 0.3989422804014327
    return (before * half).astype(BF16), half + before * density


class Weights:
    def __init__(self, refs, places, buffer, sems, slope=None, slopes=None):
        self.places = places
        self.ahead = len(places) if slope is None else 3
        self.copies = []
        for at, (ref, group) in enumerate(zip(refs, places)):
            copies = [pltpu.make_async_copy(ref, buffer.at[group], sems.at[at])]
            if slope is not None:
                copies.append(
                    pltpu.make_async_copy(
                        slope.at[group], slopes.at[group], sems.at[MP + group]
                    )
                )
            self.copies.append(copies)
        for at in range(min(self.ahead, len(places))):
            self.start(at)

    def start(self, at):
        for copy in self.copies[at]:
            copy.start()

    def __iter__(self):
        for at, group in enumerate(self.places):
            for copy in self.copies[at]:
                copy.wait()
            if at + self.ahead < len(self.places):
                self.start(at + self.ahead)
            yield group


class Moves:
    def __init__(self, sems, base):
        self.sems, self.at, self.copies = sems, base, []

    def start(self, source, target):
        copy = pltpu.make_async_copy(source, target, self.sems.at[self.at])
        self.at += 1
        copy.start()
        self.copies.append(copy)

    def wait(self):
        for copy in self.copies:
            copy.wait()
        self.copies = []


def normalise(x, params, conv, normed_out):
    def convolve(lanes):
        conv[:, lanes] = depthwise(x[:, lanes].astype(F32), params, lanes, False)

    each_lanes(convolve)
    values = conv[...]
    mean = jnp.sum(values, axis=1, keepdims=True) * (1.0 / C)
    centered = values - mean
    var = jnp.sum(centered * centered, axis=1, keepdims=True) * (1.0 / C)
    rstd = lax.rsqrt(var + 1e-6)
    normed_out[...] = (centered * rstd * params[GAIN : GAIN + 1]).astype(BF16)
    return rstd


def expand(normed, buffer, group):
    before = dot(normed[:, :HALF_C], buffer[group, :HID, :HID])
    return before + dot(normed[:, HALF_C:], buffer[group, :HID, HID:])


WIDE = jax.ShapeDtypeStruct((TOK, C), BF16)
SUMS = jax.ShapeDtypeStruct((TOK, C), F32)
RSTD = jax.ShapeDtypeStruct((TOK, LANES), F32)
SLOPE = jax.ShapeDtypeStruct((MP, TOK, HID), F32)
SCRATCH = {
    "tokens": pltpu.VMEM((TOK, C), BF16),
    "grads": pltpu.VMEM((TOK, C), BF16),
    "branch": pltpu.VMEM((TOK, C), BF16),
    "normed_here": pltpu.VMEM((TOK, C), BF16),
    "params_here": pltpu.VMEM((PARAM_ROWS, C), F32),
    "rstd_here": pltpu.VMEM((TOK, LANES), F32),
    "total": pltpu.VMEM((TOK, C), F32),
    "slopes": pltpu.VMEM((MP, TOK, HID), F32),
    "buffer": pltpu.VMEM((MP, C, C), BF16),
    "sems": pltpu.SemaphoreType.DMA((40,)),
}


def forward_body(r, weights, places):
    loads, saves = Moves(r["sems"], 2 * MP), Moves(r["sems"], 2 * MP + 8)
    total, normed, params = r["total"], r["normed_here"], r["params_here"]
    first, save = "x" in r, "slope" in r
    if first:
        loads.start(r["x"], r["tokens"])
        loads.start(r["params"], params)
    else:
        loads.start(r["normed_in"], normed)
        loads.start(r["sums_in"], total)
    groups = Weights(weights, places, r["buffer"], r["sems"])
    loads.wait()
    if first:
        rstd = normalise(r["tokens"], params, total, normed)
        saves.start(normed, r["normed"])
        total[...] = jnp.zeros((TOK, C), F32)
    if save:
        r["rstd_here"][...] = jnp.broadcast_to(rstd, (TOK, LANES))
        saves.start(r["rstd_here"], r["rstd"])
    for group in groups:
        hidden, slope = gelu_parts(expand(normed, r["buffer"], group))
        if save:
            r["slopes"][group] = slope
            saves.start(r["slopes"].at[group], r["slope"].at[group])
        part = dot(hidden, r["buffer"][group, HID:, :])
        total[...] += part.astype(BF16).astype(F32)
    if "out" in r:
        x = r["tokens"][...].astype(F32)
        scale = params[SCALE : SCALE + 1]
        r["branch"][...] = (x + scale * total[...]).astype(BF16)
        saves.start(r["branch"], r["out"])
    elif "part" in r:
        r["branch"][...] = total[...].astype(BF16)
        saves.start(r["branch"], r["part"])
    else:
        saves.start(total, r["sums"])
    saves.wait()


def join_body(r, weights, places):
    loads, saves = Moves(r["sems"], 2 * MP), Moves(r["sems"], 2 * MP + 8)
    loads.start(r["x"], r["tokens"])
    loads.start(r["params"], r["params_here"])
    loads.start(r["mine"], r["grads"])
    loads.start(r["other"], r["normed_here"])
    loads.wait()
    mixed = r["grads"][...].astype(F32) + r["normed_here"][...].astype(F32)
    x = r["tokens"][...].astype(F32)
    scale = r["params_here"][SCALE : SCALE + 1]
    r["branch"][...] = (x + scale * mixed).astype(BF16)
    saves.start(r["branch"], r["out"])
    saves.wait()


def pull_back(r, groups, rstd):
    g, params, total, branch = r["grads"], r["params_here"], r["total"], r["branch"]
    branch[...] = (g[...].astype(F32) * params[SCALE : SCALE + 1]).astype(BF16)
    total[...] = jnp.zeros((TOK, C), F32)
    for group in groups:
        spread = dot(branch[...], r["buffer"][group, HID:, :], ((1,), (1,)))
        back = (spread * r["slopes"][group]).astype(BF16)
        for half in range(2):
            lanes = slice(half * HALF_C, (half + 1) * HALF_C)
            part = dot(back, r["buffer"][group, :HID, lanes], ((1,), (1,)))
            total[:, lanes] += part.astype(BF16).astype(F32)
    inner = total[...] * params[GAIN : GAIN + 1]
    xhat = r["normed_here"][...].astype(F32) * params[INVERSE : INVERSE + 1]
    first = jnp.sum(inner, axis=1, keepdims=True) * (1.0 / C)
    second = jnp.sum(inner * xhat, axis=1, keepdims=True) * (1.0 / C)
    total[...] = (inner - first - xhat * second) * rstd

    def convolve(lanes):
        value = depthwise(total[:, lanes], params, lanes, True)
        branch[:, lanes] = (g[:, lanes].astype(F32) + value).astype(BF16)

    each_lanes(convolve)


def backward_body(r, weights, places):
    loads, saves = Moves(r["sems"], 2 * MP), Moves(r["sems"], 2 * MP + 8)
    loads.start(r["g"], r["grads"])
    loads.start(r["params"], r["params_here"])
    loads.start(r["normed_in"], r["normed_here"])
    loads.start(r["rstd_in"], r["rstd_here"])
    groups = Weights(
        weights, places, r["buffer"], r["sems"], r["slope_in"], r["slopes"]
    )
    loads.wait()
    pull_back(r, groups, r["rstd_here"][:, :1])
    saves.start(r["branch"], r["out"])
    saves.wait()


def turn_body(r, weights, places):
    loads, saves = Moves(r["sems"], 2 * MP), Moves(r["sems"], 2 * MP + 8)
    loads.start(r["x"], r["tokens"])
    loads.start(r["params"], r["params_here"])
    loads.start(r["g"], r["grads"])
    groups = Weights(weights, places, r["buffer"], r["sems"])
    loads.wait()
    rstd = normalise(r["tokens"], r["params_here"], r["total"], r["normed_here"])
    saves.start(r["normed_here"], r["normed"])
    for group in groups:
        r["slopes"][group] = gelu_parts(expand(r["normed_here"], r["buffer"], group))[1]
    pull_back(r, range(MP), rstd)
    saves.start(r["branch"], r["out"])
    saves.wait()


def block_kernel(body, names, places, sc, *refs):
    r = dict(zip(names, refs))

    @pl.when(sc[0] == 1)
    def _():
        body(r, [r[at] for at in range(len(places))], places)


def call_block(body, active, operands, weights, places, outs):
    anywhere = pl.BlockSpec(memory_space=pl.ANY)
    pieces = len(weights)
    names = list(operands) + list(range(pieces)) + list(outs) + list(SCRATCH)
    results = pl.pallas_call(
        functools.partial(block_kernel, body, names, places),
        in_specs=[pl.BlockSpec(memory_space=pltpu.SMEM)]
        + [anywhere] * (len(operands) + pieces),
        out_specs=[anywhere] * len(outs),
        out_shape=list(outs.values()),
        scratch_shapes=list(SCRATCH.values()),
        cost_estimate=pl.CostEstimate(
            flops=4 * TOK * C * HID * max(pieces, 1),
            bytes_accessed=2 * C * C * max(pieces, 1),
            transcendentals=0,
        ),
        compiler_params=SMALL,
    )(active, *operands.values(), *weights)
    return dict(zip(outs, results))


def grads_kernel(sc, recv, other, scale, w_in, w_out, keep, give):
    early_here, late_here, core = sc[0], sc[1], sc[2]
    shares = [ref[k] for ref in (recv, other) for k in range(CHIPS)]
    normed = jnp.concatenate([share[:HALF] for share in shares], axis=0)
    g = jnp.concatenate([share[HALF:] for share in shares], axis=0)
    branch = (g.astype(F32) * scale[...]).astype(BF16)
    hidden, slope = gelu_parts(dot(normed, w_in[...]))
    back = (dot(branch, w_out[...], ((1,), (1,))) * slope).astype(BF16)
    for half in range(2):
        lanes = slice(half * HALF_C, (half + 1) * HALF_C)
        gin = dot(normed[:, lanes], back, ((0,), (0,))).astype(BF16)
        gout = dot(branch[:, lanes], hidden, ((0,), (0,))).astype(BF16)
        for part in range(DP // 2):
            rows = slice(part * OUT_ROWS, (part + 1) * OUT_ROWS)
            block = jnp.concatenate([gin[rows], gout[rows]], axis=1)
            owner = half * (DP // 2) + part
            low, high = owner % 2, owner % SIDE // 2
            early = jnp.where(core == 0, low, high)
            late = jnp.where(core == 0, high, low)
            slot = jnp.where(late == late_here, 0, SIDE) + owner // SIDE

            @pl.when(early == early_here)
            def _():
                keep[slot] = block

            @pl.when(early != early_here)
            def _():
                give[slot] = block


def run_grads(sc, recv, other, scale, w_in, w_out):
    vmem = pl.BlockSpec(memory_space=pltpu.VMEM)
    eight = jax.ShapeDtypeStruct((DP // 2, OUT_ROWS, 2 * HID), BF16)
    return pl.pallas_call(
        grads_kernel,
        in_specs=[pl.BlockSpec(memory_space=pltpu.SMEM)] + [vmem] * 5,
        out_specs=[vmem] * 2,
        out_shape=[eight, eight],
        compiler_params=SMALL,
    )(sc, recv, other, scale, w_in, w_out)


def sum_over_dp(keep, give):
    add = lambda a, b: (a.astype(F32) + b.astype(F32)).astype(BF16)
    trade = lambda v, by: lax.ppermute(
        v,
        ("dp", "mp"),
        [(z * MP + j, (z ^ by[j % 2]) * MP + j) for z in range(DP) for j in range(MP)],
    )
    value = add(keep, trade(give, (1, 2)))
    value = add(value[:SIDE], trade(value[SIDE:], (2, 1)))
    here = lax.axis_index("dp") // SIDE
    block = lambda ahead: lax.dynamic_index_in_dim(
        value, (here + ahead) % SIDE, 0, keepdims=False
    )
    total = block(0).astype(F32)
    for ahead in range(1, SIDE):
        pairs = [(z, (z + ahead * SIDE) % DP) for z in range(DP)]
        total = total + lax.ppermute(block(ahead), "dp", pairs).astype(F32)
    return total.astype(BF16)


def shards(images, token_grads, counts, dw_kernel, ln_gain, w_in, w_out, layer_scale):
    s = lax.axis_index("section")
    j = lax.axis_index("mp")
    chip, core = j // 2, j % 2
    w_in, w_out = w_in[0], w_out[0]

    up = [(i, (i + 2) % MP) for i in range(MP)]
    down = [(i, (i - 2) % MP) for i in range(MP)]
    swap = [(i, i ^ 1) for i in range(MP)]
    move = lambda v, pairs: lax.ppermute(v, "mp", pairs)
    own = jnp.concatenate(
        [jnp.concatenate([w_in[:HALF_C], w_in[HALF_C:]], axis=1), w_out], axis=0
    )
    sample, image = chip // 2, chip % 2
    live = (image < lax.dynamic_index_in_dim(counts, sample, 0, keepdims=False)).astype(BF16)
    one = lambda v: (
        lax.dynamic_index_in_dim(
            v.reshape((CHIPS,) + v.shape[2:]), chip, 0, keepdims=False
        )
        * live
    ).transpose(1, 0, 2).reshape(TOK, C)

    x, g = one(images), one(token_grads)
    params = jnp.concatenate(
        [
            dw_kernel.reshape(TAP_ROWS, C),
            ln_gain,
            layer_scale,
            1.0 / ln_gain,
            jnp.zeros((PARAM_ROWS - TAP_ROWS - 3, C), F32),
        ]
    )
    around = [(i, (i + 2 - 4 * (i % 2)) % MP) for i in range(MP)]
    counter = [(i, (i - 2 + 4 * (i % 2)) % MP) for i in range(MP)]
    first = move(own, around)
    first, own, x, g, params = lax.optimization_barrier((first, own, x, g, params))
    second = move(own, counter)
    third = move(first, around)

    active = [(s == block).astype(jnp.int32)[None] for block in range(DEPTH)]
    send = lambda v, source, to: lax.ppermute(v, "section", [(source, to)])

    result = call_block(
        forward_body,
        active[0],
        dict(x=x, params=params),
        [own, first],
        [0, 1],
        dict(normed=WIDE, sums=SUMS),
    )
    normed = result["normed"]
    swap_own, swap_first, sums = lax.optimization_barrier((own, first, result["sums"]))
    result = call_block(
        forward_body,
        active[0],
        dict(normed_in=normed, sums_in=sums),
        [second, third],
        [0, 1],
        dict(part=WIDE),
    )
    swap_second, swap_third, part = lax.optimization_barrier((second, third, result["part"]))
    result = call_block(
        join_body,
        active[0],
        dict(x=x, params=params, mine=part, other=move(part, swap)),
        [],
        [],
        dict(out=WIDE),
    )
    out = result["out"]

    weights = [own, first, move(swap_own, swap), move(swap_first, swap)]
    weights += [second, third, move(swap_second, swap), move(swap_third, swap)]
    places = list(range(MP))
    normed_of, saved = [normed], [None]
    for block in range(1, DEPTH - 1):
        result = call_block(
            forward_body,
            active[block],
            dict(x=send(out, block - 1, block), params=params),
            weights,
            places,
            dict(out=WIDE, normed=WIDE, rstd=RSTD, slope=SLOPE),
        )
        out = result["out"]
        normed_of.append(result["normed"])
        saved.append(result)
    result = call_block(
        turn_body,
        active[DEPTH - 1],
        dict(x=send(out, DEPTH - 2, DEPTH - 1), g=g, params=params),
        weights,
        places,
        dict(out=WIDE, normed=WIDE),
    )
    normed_of.append(result["normed"])
    g_of = [g]
    for block in range(DEPTH - 2, 0, -1):
        g = send(result["out"], block + 1, block)
        g_of.append(g)
        kept = saved[block]
        result = call_block(
            backward_body,
            active[block],
            dict(
                g=g,
                params=params,
                normed_in=kept["normed"],
                rstd_in=kept["rstd"],
                slope_in=kept["slope"],
            ),
            weights,
            places,
            dict(out=WIDE),
        )
    g_of.append(send(result["out"], 1, 0))

    pick = lambda values: lax.select_n(s, *values)
    mine = jnp.stack([pick(normed_of), pick(g_of[::-1])])
    mine = jnp.where(core == 0, mine[:, :HALF], mine[:, HALF:]).reshape(TOK, C)
    recv = lax.all_to_all(
        jnp.broadcast_to(mine[None], (CHIPS, TOK, C)),
        "mp",
        0,
        0,
        axis_index_groups=[list(range(0, MP, 2)), list(range(1, MP, 2))],
        tiled=True,
    )
    other = move(recv, swap)
    z = lax.axis_index("dp")
    low, high = z % 2, z % SIDE // 2
    place = [jnp.where(core == 0, low, high), jnp.where(core == 0, high, low), core]
    place = jnp.stack([jnp.asarray(v, jnp.int32) for v in place])
    total = sum_over_dp(*run_grads(place, recv, other, layer_scale, w_in, w_out))
    return total[None, :, :HID], total[None, :, HID:]


def solution(mesh):
    return jax.shard_map(
        shards,
        mesh=mesh,
        in_specs=(
            P("dp", None, None, None, None),
            P("dp", None, None, None, None),
            P("dp"),
            P("section", None, None, None),
            P("section", None),
            P("section", None, "mp"),
            P("section", "mp", None),
            P("section", None),
        ),
        out_specs=(P("section", "dp", "mp"), P("section", "dp", "mp")),
        check_vma=False,
    )
```

```python
import functools

import jax
import jax.numpy as jnp
from jax import lax
from jax.experimental import pallas as pl
from jax.experimental.pallas import tpu as pltpu
from jax.sharding import PartitionSpec as P

F32 = jnp.float32
BF16 = jnp.bfloat16

MP = 8
CHIPS = 4
DP = 16
SIDE = 4
DEPTH = 4
ROWS, COLS, TAPS = 8, 12, 7
TOK = ROWS * COLS
HALF = TOK // 2
C = 768
HALF_C = C // 2
HID = 384
LANES = 128
TAP_ROWS = TAPS * TAPS
GAIN, SCALE, INVERSE, PARAM_ROWS = TAP_ROWS, TAP_ROWS + 1, TAP_ROWS + 2, 56
OUT_ROWS = C // DP
PARAMS = pltpu.CompilerParams(vmem_limit_bytes=56 * 1024 * 1024)
SMALL = pltpu.CompilerParams(vmem_limit_bytes=24 * 1024 * 1024)


def dot(a, b, contract=((1,), (0,))):
    return lax.dot_general(a, b, (contract, ((), ())), preferred_element_type=F32)


def depthwise(values, kernel_ref, lanes, flip):
    values = values.reshape(COLS, ROWS, LANES)
    row = lax.broadcasted_iota(jnp.int32, (COLS, ROWS, LANES), 1)
    edge = jnp.zeros((3, ROWS, LANES), F32)
    total = jnp.zeros((COLS, ROWS, LANES), F32)
    for a in range(TAPS):
        by = a - 3
        moved = values
        if by != 0:
            moved = pltpu.roll(moved, (-by) % ROWS, 1)
            moved = jnp.where((row + by >= 0) & (row + by < ROWS), moved, 0.0)
        wide = jnp.concatenate([edge, moved, edge], axis=0)
        for e in range(TAPS):
            at = a * TAPS + e
            if flip:
                at = TAPS * TAPS - 1 - at
            total = total + wide[e : e + COLS] * kernel_ref[at : at + 1, lanes][None]
    return total.reshape(TOK, LANES)


def each_lanes(body):
    @pl.loop(0, C // LANES)
    def _(tile):
        body(pl.ds(pl.multiple_of(tile * LANES, LANES), LANES))


def gelu_parts(before):
    half = 0.5 * (1.0 + lax.erf(before * (0.5**0.5)))
    density = jnp.exp(-0.5 * before * before) * 0.3989422804014327
    return (before * half).astype(BF16), half + before * density


class Weights:
    def __init__(self, refs, places, buffer, sems, slope=None, slopes=None):
        self.places = places
        self.ahead = len(places) if slope is None else 3
        self.copies = []
        for at, (ref, group) in enumerate(zip(refs, places)):
            copies = [pltpu.make_async_copy(ref, buffer.at[group], sems.at[at])]
            if slope is not None:
                copies.append(
                    pltpu.make_async_copy(
                        slope.at[group], slopes.at[group], sems.at[MP + group]
                    )
                )
            self.copies.append(copies)
        for at in range(min(self.ahead, len(places))):
            self.start(at)

    def start(self, at):
        for copy in self.copies[at]:
            copy.start()

    def __iter__(self):
        for at, group in enumerate(self.places):
            for copy in self.copies[at]:
                copy.wait()
            if at + self.ahead < len(self.places):
                self.start(at + self.ahead)
            yield group


class Moves:
    def __init__(self, sems, base):
        self.sems, self.at, self.copies = sems, base, []

    def start(self, source, target):
        copy = pltpu.make_async_copy(source, target, self.sems.at[self.at])
        self.at += 1
        copy.start()
        self.copies.append(copy)

    def wait(self):
        for copy in self.copies:
            copy.wait()
        self.copies = []


def normalise(x, params, conv, normed_out):
    def convolve(lanes):
        conv[:, lanes] = depthwise(x[:, lanes].astype(F32), params, lanes, False)

    each_lanes(convolve)
    values = conv[...]
    mean = jnp.sum(values, axis=1, keepdims=True) * (1.0 / C)
    centered = values - mean
    var = jnp.sum(centered * centered, axis=1, keepdims=True) * (1.0 / C)
    rstd = lax.rsqrt(var + 1e-6)
    normed_out[...] = (centered * rstd * params[GAIN : GAIN + 1]).astype(BF16)
    return rstd


def expand(normed, buffer, group):
    before = dot(normed[:, :HALF_C], buffer[group, :HID, :HID])
    return before + dot(normed[:, HALF_C:], buffer[group, :HID, HID:])


WIDE = jax.ShapeDtypeStruct((TOK, C), BF16)
SUMS = jax.ShapeDtypeStruct((TOK, C), F32)
RSTD = jax.ShapeDtypeStruct((TOK, LANES), F32)
SLOPE = jax.ShapeDtypeStruct((MP, TOK, HID), F32)
SCRATCH = {
    "tokens": pltpu.VMEM((TOK, C), BF16),
    "grads": pltpu.VMEM((TOK, C), BF16),
    "branch": pltpu.VMEM((TOK, C), BF16),
    "normed_here": pltpu.VMEM((TOK, C), BF16),
    "params_here": pltpu.VMEM((PARAM_ROWS, C), F32),
    "rstd_here": pltpu.VMEM((TOK, LANES), F32),
    "total": pltpu.VMEM((TOK, C), F32),
    "slopes": pltpu.VMEM((MP, TOK, HID), F32),
    "buffer": pltpu.VMEM((MP, C, C), BF16),
    "sems": pltpu.SemaphoreType.DMA((40,)),
}


def forward_body(r, weights, places):
    loads, saves = Moves(r["sems"], 2 * MP), Moves(r["sems"], 2 * MP + 8)
    total, normed, params = r["total"], r["normed_here"], r["params_here"]
    first, save = "x" in r, "slope" in r
    if first:
        loads.start(r["x"], r["tokens"])
        loads.start(r["params"], params)
    else:
        loads.start(r["normed_in"], normed)
        loads.start(r["sums_in"], total)
    groups = Weights(weights, places, r["buffer"], r["sems"])
    loads.wait()
    if first:
        rstd = normalise(r["tokens"], params, total, normed)
        saves.start(normed, r["normed"])
        total[...] = jnp.zeros((TOK, C), F32)
    if save:
        r["rstd_here"][...] = jnp.broadcast_to(rstd, (TOK, LANES))
        saves.start(r["rstd_here"], r["rstd"])
    for group in groups:
        hidden, slope = gelu_parts(expand(normed, r["buffer"], group))
        if save:
            r["slopes"][group] = slope
            saves.start(r["slopes"].at[group], r["slope"].at[group])
        part = dot(hidden, r["buffer"][group, HID:, :])
        total[...] += part.astype(BF16).astype(F32)
    if "out" in r:
        x = r["tokens"][...].astype(F32)
        scale = params[SCALE : SCALE + 1]
        r["branch"][...] = (x + scale * total[...]).astype(BF16)
        saves.start(r["branch"], r["out"])
    elif "part" in r:
        r["branch"][...] = total[...].astype(BF16)
        saves.start(r["branch"], r["part"])
    else:
        saves.start(total, r["sums"])
    saves.wait()


def join_body(r, weights, places):
    loads, saves = Moves(r["sems"], 2 * MP), Moves(r["sems"], 2 * MP + 8)
    loads.start(r["x"], r["tokens"])
    loads.start(r["params"], r["params_here"])
    loads.start(r["mine"], r["grads"])
    loads.start(r["other"], r["normed_here"])
    loads.wait()
    mixed = r["grads"][...].astype(F32) + r["normed_here"][...].astype(F32)
    x = r["tokens"][...].astype(F32)
    scale = r["params_here"][SCALE : SCALE + 1]
    r["branch"][...] = (x + scale * mixed).astype(BF16)
    saves.start(r["branch"], r["out"])
    saves.wait()


def pull_back(r, groups, rstd):
    g, params, total, branch = r["grads"], r["params_here"], r["total"], r["branch"]
    branch[...] = (g[...].astype(F32) * params[SCALE : SCALE + 1]).astype(BF16)
    total[...] = jnp.zeros((TOK, C), F32)
    for group in groups:
        spread = dot(branch[...], r["buffer"][group, HID:, :], ((1,), (1,)))
        back = (spread * r["slopes"][group]).astype(BF16)
        for half in range(2):
            lanes = slice(half * HALF_C, (half + 1) * HALF_C)
            part = dot(back, r["buffer"][group, :HID, lanes], ((1,), (1,)))
            total[:, lanes] += part.astype(BF16).astype(F32)
    inner = total[...] * params[GAIN : GAIN + 1]
    xhat = r["normed_here"][...].astype(F32) * params[INVERSE : INVERSE + 1]
    first = jnp.sum(inner, axis=1, keepdims=True) * (1.0 / C)
    second = jnp.sum(inner * xhat, axis=1, keepdims=True) * (1.0 / C)
    total[...] = (inner - first - xhat * second) * rstd

    def convolve(lanes):
        value = depthwise(total[:, lanes], params, lanes, True)
        branch[:, lanes] = (g[:, lanes].astype(F32) + value).astype(BF16)

    each_lanes(convolve)


def backward_body(r, weights, places):
    loads, saves = Moves(r["sems"], 2 * MP), Moves(r["sems"], 2 * MP + 8)
    loads.start(r["g"], r["grads"])
    loads.start(r["params"], r["params_here"])
    loads.start(r["normed_in"], r["normed_here"])
    loads.start(r["rstd_in"], r["rstd_here"])
    groups = Weights(
        weights, places, r["buffer"], r["sems"], r["slope_in"], r["slopes"]
    )
    loads.wait()
    pull_back(r, groups, r["rstd_here"][:, :1])
    saves.start(r["branch"], r["out"])
    saves.wait()


def turn_body(r, weights, places):
    loads, saves = Moves(r["sems"], 2 * MP), Moves(r["sems"], 2 * MP + 8)
    loads.start(r["x"], r["tokens"])
    loads.start(r["params"], r["params_here"])
    loads.start(r["g"], r["grads"])
    groups = Weights(weights, places, r["buffer"], r["sems"])
    loads.wait()
    rstd = normalise(r["tokens"], r["params_here"], r["total"], r["normed_here"])
    saves.start(r["normed_here"], r["normed"])
    for group in groups:
        r["slopes"][group] = gelu_parts(expand(r["normed_here"], r["buffer"], group))[1]
    pull_back(r, range(MP), rstd)
    saves.start(r["branch"], r["out"])
    saves.wait()


def block_kernel(body, names, places, sc, *refs):
    r = dict(zip(names, refs))

    @pl.when(sc[0] == 1)
    def _():
        body(r, [r[at] for at in range(len(places))], places)


def call_block(body, active, operands, weights, places, outs):
    anywhere = pl.BlockSpec(memory_space=pl.ANY)
    pieces = len(weights)
    names = list(operands) + list(range(pieces)) + list(outs) + list(SCRATCH)
    results = pl.pallas_call(
        functools.partial(block_kernel, body, names, places),
        in_specs=[pl.BlockSpec(memory_space=pltpu.SMEM)]
        + [anywhere] * (len(operands) + pieces),
        out_specs=[anywhere] * len(outs),
        out_shape=list(outs.values()),
        scratch_shapes=list(SCRATCH.values()),
        cost_estimate=pl.CostEstimate(
            flops=4 * TOK * C * HID * max(pieces, 1),
            bytes_accessed=2 * C * C * max(pieces, 1),
            transcendentals=0,
        ),
        compiler_params=SMALL if pieces < MP else PARAMS,
    )(active, *operands.values(), *weights)
    return dict(zip(outs, results))


def grads_kernel(sc, recv, other, scale, w_in, w_out, keep, give):
    early_here, late_here, core = sc[0], sc[1], sc[2]
    shares = [ref[k] for ref in (recv, other) for k in range(CHIPS)]
    normed = jnp.concatenate([share[:HALF] for share in shares], axis=0)
    g = jnp.concatenate([share[HALF:] for share in shares], axis=0)
    branch = (g.astype(F32) * scale[...]).astype(BF16)
    hidden, slope = gelu_parts(dot(normed, w_in[...]))
    back = (dot(branch, w_out[...], ((1,), (1,))) * slope).astype(BF16)
    for half in range(2):
        lanes = slice(half * HALF_C, (half + 1) * HALF_C)
        gin = dot(normed[:, lanes], back, ((0,), (0,))).astype(BF16)
        gout = dot(branch[:, lanes], hidden, ((0,), (0,))).astype(BF16)
        for part in range(DP // 2):
            rows = slice(part * OUT_ROWS, (part + 1) * OUT_ROWS)
            block = jnp.concatenate([gin[rows], gout[rows]], axis=1)
            owner = half * (DP // 2) + part
            low, high = owner % 2, owner % SIDE // 2
            early = jnp.where(core == 0, low, high)
            late = jnp.where(core == 0, high, low)
            slot = jnp.where(late == late_here, 0, SIDE) + owner // SIDE

            @pl.when(early == early_here)
            def _():
                keep[slot] = block

            @pl.when(early != early_here)
            def _():
                give[slot] = block


def run_grads(sc, recv, other, scale, w_in, w_out):
    vmem = pl.BlockSpec(memory_space=pltpu.VMEM)
    eight = jax.ShapeDtypeStruct((DP // 2, OUT_ROWS, 2 * HID), BF16)
    return pl.pallas_call(
        grads_kernel,
        in_specs=[pl.BlockSpec(memory_space=pltpu.SMEM)] + [vmem] * 5,
        out_specs=[vmem] * 2,
        out_shape=[eight, eight],
        compiler_params=SMALL,
    )(sc, recv, other, scale, w_in, w_out)


def sum_over_dp(keep, give):
    add = lambda a, b: (a.astype(F32) + b.astype(F32)).astype(BF16)
    trade = lambda v, by: lax.ppermute(
        v,
        ("dp", "mp"),
        [(z * MP + j, (z ^ by[j % 2]) * MP + j) for z in range(DP) for j in range(MP)],
    )
    value = add(keep, trade(give, (1, 2)))
    value = add(value[:SIDE], trade(value[SIDE:], (2, 1)))
    here = lax.axis_index("dp") // SIDE
    block = lambda ahead: lax.dynamic_index_in_dim(
        value, (here + ahead) % SIDE, 0, keepdims=False
    )
    total = block(0).astype(F32)
    for ahead in range(1, SIDE):
        pairs = [(z, (z + ahead * SIDE) % DP) for z in range(DP)]
        total = total + lax.ppermute(block(ahead), "dp", pairs).astype(F32)
    return total.astype(BF16)


def shards(images, token_grads, counts, dw_kernel, ln_gain, w_in, w_out, layer_scale):
    s = lax.axis_index("section")
    j = lax.axis_index("mp")
    chip, core = j // 2, j % 2
    w_in, w_out = w_in[0], w_out[0]

    up = [(i, (i + 2) % MP) for i in range(MP)]
    down = [(i, (i - 2) % MP) for i in range(MP)]
    swap = [(i, i ^ 1) for i in range(MP)]
    move = lambda v, pairs: lax.ppermute(v, "mp", pairs)
    own = jnp.concatenate(
        [jnp.concatenate([w_in[:HALF_C], w_in[HALF_C:]], axis=1), w_out], axis=0
    )
    sample, image = chip // 2, chip % 2
    live = (image < lax.dynamic_index_in_dim(counts, sample, 0, keepdims=False)).astype(BF16)
    one = lambda v: (
        lax.dynamic_index_in_dim(
            v.reshape((CHIPS,) + v.shape[2:]), chip, 0, keepdims=False
        )
        * live
    ).transpose(1, 0, 2).reshape(TOK, C)

    x, g = one(images), one(token_grads)
    params = jnp.concatenate(
        [
            dw_kernel.reshape(TAP_ROWS, C),
            ln_gain,
            layer_scale,
            1.0 / ln_gain,
            jnp.zeros((PARAM_ROWS - TAP_ROWS - 3, C), F32),
        ]
    )
    around = [(i, (i + 2 - 4 * (i % 2)) % MP) for i in range(MP)]
    counter = [(i, (i - 2 + 4 * (i % 2)) % MP) for i in range(MP)]
    first = move(own, around)
    first, own, x, g, params = lax.optimization_barrier((first, own, x, g, params))
    second = move(own, counter)
    third = move(first, around)

    active = [(s == block).astype(jnp.int32)[None] for block in range(DEPTH)]
    send = lambda v, source, to: lax.ppermute(v, "section", [(source, to)])

    result = call_block(
        forward_body,
        active[0],
        dict(x=x, params=params),
        [own, first],
        [0, 1],
        dict(normed=WIDE, sums=SUMS),
    )
    normed = result["normed"]
    swap_own, swap_first, sums = lax.optimization_barrier((own, first, result["sums"]))
    result = call_block(
        forward_body,
        active[0],
        dict(normed_in=normed, sums_in=sums),
        [second, third],
        [0, 1],
        dict(part=WIDE),
    )
    swap_second, swap_third, part = lax.optimization_barrier((second, third, result["part"]))
    result = call_block(
        join_body,
        active[0],
        dict(x=x, params=params, mine=part, other=move(part, swap)),
        [],
        [],
        dict(out=WIDE),
    )
    out = result["out"]

    weights = [own, first, move(swap_own, swap), move(swap_first, swap)]
    weights += [second, third, move(swap_second, swap), move(swap_third, swap)]
    places = list(range(MP))
    normed_of, saved = [normed], [None]
    for block in range(1, DEPTH - 1):
        result = call_block(
            forward_body,
            active[block],
            dict(x=send(out, block - 1, block), params=params),
            weights,
            places,
            dict(out=WIDE, normed=WIDE, rstd=RSTD, slope=SLOPE),
        )
        out = result["out"]
        normed_of.append(result["normed"])
        saved.append(result)
    result = call_block(
        turn_body,
        active[DEPTH - 1],
        dict(x=send(out, DEPTH - 2, DEPTH - 1), g=g, params=params),
        weights,
        places,
        dict(out=WIDE, normed=WIDE),
    )
    normed_of.append(result["normed"])
    g_of = [g]
    for block in range(DEPTH - 2, 0, -1):
        g = send(result["out"], block + 1, block)
        g_of.append(g)
        kept = saved[block]
        result = call_block(
            backward_body,
            active[block],
            dict(
                g=g,
                params=params,
                normed_in=kept["normed"],
                rstd_in=kept["rstd"],
                slope_in=kept["slope"],
            ),
            weights,
            places,
            dict(out=WIDE),
        )
    g_of.append(send(result["out"], 1, 0))

    pick = lambda values: lax.select_n(s, *values)
    mine = jnp.stack([pick(normed_of), pick(g_of[::-1])])
    mine = jnp.where(core == 0, mine[:, :HALF], mine[:, HALF:]).reshape(TOK, C)
    recv = lax.all_to_all(
        jnp.broadcast_to(mine[None], (CHIPS, TOK, C)),
        "mp",
        0,
        0,
        axis_index_groups=[list(range(0, MP, 2)), list(range(1, MP, 2))],
        tiled=True,
    )
    other = move(recv, swap)
    z = lax.axis_index("dp")
    low, high = z % 2, z % SIDE // 2
    place = [jnp.where(core == 0, low, high), jnp.where(core == 0, high, low), core]
    place = jnp.stack([jnp.asarray(v, jnp.int32) for v in place])
    total = sum_over_dp(*run_grads(place, recv, other, layer_scale, w_in, w_out))
    return total[None, :, :HID], total[None, :, HID:]


def solution(mesh):
    return jax.shard_map(
        shards,
        mesh=mesh,
        in_specs=(
            P("dp", None, None, None, None),
            P("dp", None, None, None, None),
            P("dp"),
            P("section", None, None, None),
            P("section", None),
            P("section", None, "mp"),
            P("section", "mp", None),
            P("section", None),
        ),
        out_specs=(P("section", "dp", "mp"), P("section", "dp", "mp")),
        check_vma=False,
    )
```

```python
import functools

import jax
import jax.numpy as jnp
from jax import lax
from jax.experimental import pallas as pl
from jax.experimental.pallas import tpu as pltpu
from jax.sharding import PartitionSpec as P

F32 = jnp.float32
BF16 = jnp.bfloat16

MP = 8
CHIPS = 4
DP = 16
SIDE = 4
DEPTH = 4
ROWS, COLS, TAPS = 8, 12, 7
TOK = ROWS * COLS
HALF = TOK // 2
C = 768
HALF_C = C // 2
HID = 384
LANES = 128
TAP_ROWS = TAPS * TAPS
GAIN, SCALE, INVERSE, PARAM_ROWS = TAP_ROWS, TAP_ROWS + 1, TAP_ROWS + 2, 56
OUT_ROWS = C // DP
PARAMS = pltpu.CompilerParams(vmem_limit_bytes=56 * 1024 * 1024)
SMALL = pltpu.CompilerParams(vmem_limit_bytes=24 * 1024 * 1024)


def dot(a, b, contract=((1,), (0,))):
    return lax.dot_general(a, b, (contract, ((), ())), preferred_element_type=F32)


def depthwise(values, kernel_ref, lanes, flip):
    values = values.reshape(COLS, ROWS, LANES)
    row = lax.broadcasted_iota(jnp.int32, (COLS, ROWS, LANES), 1)
    edge = jnp.zeros((3, ROWS, LANES), F32)
    total = jnp.zeros((COLS, ROWS, LANES), F32)
    for a in range(TAPS):
        by = a - 3
        moved = values
        if by != 0:
            moved = pltpu.roll(moved, (-by) % ROWS, 1)
            moved = jnp.where((row + by >= 0) & (row + by < ROWS), moved, 0.0)
        wide = jnp.concatenate([edge, moved, edge], axis=0)
        for e in range(TAPS):
            at = a * TAPS + e
            if flip:
                at = TAPS * TAPS - 1 - at
            total = total + wide[e : e + COLS] * kernel_ref[at : at + 1, lanes][None]
    return total.reshape(TOK, LANES)


def each_lanes(body):
    @pl.loop(0, C // LANES)
    def _(tile):
        body(pl.ds(pl.multiple_of(tile * LANES, LANES), LANES))


def gelu_parts(before):
    half = 0.5 * (1.0 + lax.erf(before * (0.5**0.5)))
    density = jnp.exp(-0.5 * before * before) * 0.3989422804014327
    return (before * half).astype(BF16), half + before * density


class Weights:
    def __init__(self, refs, places, buffer, sems, slope=None, slopes=None):
        self.places = places
        self.ahead = len(places) if slope is None else 5
        self.copies = []
        for at, (ref, group) in enumerate(zip(refs, places)):
            copies = []
            for half, sem in ((1, 40 + at), (0, at)):
                rows = pl.ds(half * HID, HID)
                copies.append(
                    pltpu.make_async_copy(ref.at[rows], buffer.at[group, rows], sems.at[sem])
                )
            if slope is not None:
                copies.append(
                    pltpu.make_async_copy(
                        slope.at[group], slopes.at[group], sems.at[MP + group]
                    )
                )
            self.copies.append(copies)
        for at in range(min(self.ahead, len(places))):
            self.start(at)

    def start(self, at):
        for copy in self.copies[at]:
            copy.start()

    def __iter__(self):
        for at, group in enumerate(self.places):
            for copy in self.copies[at]:
                copy.wait()
            if at + self.ahead < len(self.places):
                self.start(at + self.ahead)
            yield group


class Moves:
    def __init__(self, sems, base):
        self.sems, self.at, self.copies = sems, base, []

    def start(self, source, target):
        copy = pltpu.make_async_copy(source, target, self.sems.at[self.at])
        self.at += 1
        copy.start()
        self.copies.append(copy)

    def wait(self):
        for copy in self.copies:
            copy.wait()
        self.copies = []


def normalise(x, params, conv, normed_out):
    def convolve(lanes):
        conv[:, lanes] = depthwise(x[:, lanes].astype(F32), params, lanes, False)

    each_lanes(convolve)
    values = conv[...]
    mean = jnp.sum(values, axis=1, keepdims=True) * (1.0 / C)
    centered = values - mean
    var = jnp.sum(centered * centered, axis=1, keepdims=True) * (1.0 / C)
    rstd = lax.rsqrt(var + 1e-6)
    normed_out[...] = (centered * rstd * params[GAIN : GAIN + 1]).astype(BF16)
    return rstd


def expand(normed, buffer, group):
    before = dot(normed[:, :HALF_C], buffer[group, :HID, :HID])
    return before + dot(normed[:, HALF_C:], buffer[group, :HID, HID:])


WIDE = jax.ShapeDtypeStruct((TOK, C), BF16)
SUMS = jax.ShapeDtypeStruct((TOK, C), F32)
RSTD = jax.ShapeDtypeStruct((TOK, LANES), F32)
SLOPE = jax.ShapeDtypeStruct((MP, TOK, HID), F32)
SCRATCH = {
    "tokens": pltpu.VMEM((TOK, C), BF16),
    "grads": pltpu.VMEM((TOK, C), BF16),
    "branch": pltpu.VMEM((TOK, C), BF16),
    "normed_here": pltpu.VMEM((TOK, C), BF16),
    "params_here": pltpu.VMEM((PARAM_ROWS, C), F32),
    "rstd_here": pltpu.VMEM((TOK, LANES), F32),
    "total": pltpu.VMEM((TOK, C), F32),
    "slopes": pltpu.VMEM((MP, TOK, HID), F32),
    "buffer": pltpu.VMEM((MP, C, C), BF16),
    "sems": pltpu.SemaphoreType.DMA((48,)),
}


def forward_body(r, weights, places):
    loads, saves = Moves(r["sems"], 2 * MP), Moves(r["sems"], 2 * MP + 8)
    total, normed, params = r["total"], r["normed_here"], r["params_here"]
    first, save = "x" in r, "slope" in r
    if first:
        loads.start(r["x"], r["tokens"])
        loads.start(r["params"], params)
    else:
        loads.start(r["normed_in"], normed)
        loads.start(r["sums_in"], total)
    groups = Weights(weights, places, r["buffer"], r["sems"])
    loads.wait()
    if first:
        rstd = normalise(r["tokens"], params, total, normed)
        saves.start(normed, r["normed"])
        total[...] = jnp.zeros((TOK, C), F32)
    if save:
        r["rstd_here"][...] = jnp.broadcast_to(rstd, (TOK, LANES))
        saves.start(r["rstd_here"], r["rstd"])
    for group in groups:
        hidden, slope = gelu_parts(expand(normed, r["buffer"], group))
        if save:
            r["slopes"][group] = slope
            saves.start(r["slopes"].at[group], r["slope"].at[group])
        part = dot(hidden, r["buffer"][group, HID:, :])
        total[...] += part.astype(BF16).astype(F32)
    if "out" in r:
        x = r["tokens"][...].astype(F32)
        scale = params[SCALE : SCALE + 1]
        r["branch"][...] = (x + scale * total[...]).astype(BF16)
        saves.start(r["branch"], r["out"])
    elif "part" in r:
        r["branch"][...] = total[...].astype(BF16)
        saves.start(r["branch"], r["part"])
    else:
        saves.start(total, r["sums"])
    saves.wait()


def join_body(r, weights, places):
    loads, saves = Moves(r["sems"], 2 * MP), Moves(r["sems"], 2 * MP + 8)
    loads.start(r["x"], r["tokens"])
    loads.start(r["params"], r["params_here"])
    loads.start(r["mine"], r["grads"])
    loads.start(r["other"], r["normed_here"])
    loads.wait()
    mixed = r["grads"][...].astype(F32) + r["normed_here"][...].astype(F32)
    x = r["tokens"][...].astype(F32)
    scale = r["params_here"][SCALE : SCALE + 1]
    r["branch"][...] = (x + scale * mixed).astype(BF16)
    saves.start(r["branch"], r["out"])
    saves.wait()


def pull_back(r, groups, rstd):
    g, params, total, branch = r["grads"], r["params_here"], r["total"], r["branch"]
    branch[...] = (g[...].astype(F32) * params[SCALE : SCALE + 1]).astype(BF16)
    total[...] = jnp.zeros((TOK, C), F32)
    for group in groups:
        spread = dot(branch[...], r["buffer"][group, HID:, :], ((1,), (1,)))
        back = (spread * r["slopes"][group]).astype(BF16)
        for half in range(2):
            lanes = slice(half * HALF_C, (half + 1) * HALF_C)
            part = dot(back, r["buffer"][group, :HID, lanes], ((1,), (1,)))
            total[:, lanes] += part.astype(BF16).astype(F32)
    inner = total[...] * params[GAIN : GAIN + 1]
    xhat = r["normed_here"][...].astype(F32) * params[INVERSE : INVERSE + 1]
    first = jnp.sum(inner, axis=1, keepdims=True) * (1.0 / C)
    second = jnp.sum(inner * xhat, axis=1, keepdims=True) * (1.0 / C)
    total[...] = (inner - first - xhat * second) * rstd

    def convolve(lanes):
        value = depthwise(total[:, lanes], params, lanes, True)
        branch[:, lanes] = (g[:, lanes].astype(F32) + value).astype(BF16)

    each_lanes(convolve)


def backward_body(r, weights, places):
    loads, saves = Moves(r["sems"], 2 * MP), Moves(r["sems"], 2 * MP + 8)
    loads.start(r["g"], r["grads"])
    loads.start(r["params"], r["params_here"])
    loads.start(r["normed_in"], r["normed_here"])
    loads.start(r["rstd_in"], r["rstd_here"])
    groups = Weights(
        weights, places, r["buffer"], r["sems"], r["slope_in"], r["slopes"]
    )
    loads.wait()
    pull_back(r, groups, r["rstd_here"][:, :1])
    saves.start(r["branch"], r["out"])
    saves.wait()


def turn_body(r, weights, places):
    loads, saves = Moves(r["sems"], 2 * MP), Moves(r["sems"], 2 * MP + 8)
    loads.start(r["x"], r["tokens"])
    loads.start(r["params"], r["params_here"])
    loads.start(r["g"], r["grads"])
    groups = Weights(weights, places, r["buffer"], r["sems"])
    loads.wait()
    rstd = normalise(r["tokens"], r["params_here"], r["total"], r["normed_here"])
    saves.start(r["normed_here"], r["normed"])
    for group in groups:
        r["slopes"][group] = gelu_parts(expand(r["normed_here"], r["buffer"], group))[1]
    pull_back(r, range(MP), rstd)
    saves.start(r["branch"], r["out"])
    saves.wait()


def block_kernel(body, names, places, sc, *refs):
    r = dict(zip(names, refs))

    @pl.when(sc[0] == 1)
    def _():
        body(r, [r[at] for at in range(len(places))], places)


def call_block(body, active, operands, weights, places, outs):
    anywhere = pl.BlockSpec(memory_space=pl.ANY)
    pieces = len(weights)
    names = list(operands) + list(range(pieces)) + list(outs) + list(SCRATCH)
    results = pl.pallas_call(
        functools.partial(block_kernel, body, names, places),
        in_specs=[pl.BlockSpec(memory_space=pltpu.SMEM)]
        + [anywhere] * (len(operands) + pieces),
        out_specs=[anywhere] * len(outs),
        out_shape=list(outs.values()),
        scratch_shapes=list(SCRATCH.values()),
        cost_estimate=pl.CostEstimate(
            flops=4 * TOK * C * HID * max(pieces, 1),
            bytes_accessed=2 * C * C * max(pieces, 1),
            transcendentals=0,
        ),
        compiler_params=SMALL if pieces < MP else PARAMS,
    )(active, *operands.values(), *weights)
    return dict(zip(outs, results))


def grads_kernel(sc, recv, other, scale, w_in, w_out, keep, give):
    early_here, late_here, core = sc[0], sc[1], sc[2]
    shares = [ref[k] for ref in (recv, other) for k in range(CHIPS)]
    normed = jnp.concatenate([share[:HALF] for share in shares], axis=0)
    g = jnp.concatenate([share[HALF:] for share in shares], axis=0)
    branch = (g.astype(F32) * scale[...]).astype(BF16)
    hidden, slope = gelu_parts(dot(normed, w_in[...]))
    back = (dot(branch, w_out[...], ((1,), (1,))) * slope).astype(BF16)
    for half in range(2):
        lanes = slice(half * HALF_C, (half + 1) * HALF_C)
        gin = dot(normed[:, lanes], back, ((0,), (0,))).astype(BF16)
        gout = dot(branch[:, lanes], hidden, ((0,), (0,))).astype(BF16)
        for part in range(DP // 2):
            rows = slice(part * OUT_ROWS, (part + 1) * OUT_ROWS)
            block = jnp.concatenate([gin[rows], gout[rows]], axis=1)
            owner = half * (DP // 2) + part
            low, high = owner % 2, owner % SIDE // 2
            early = jnp.where(core == 0, low, high)
            late = jnp.where(core == 0, high, low)
            slot = jnp.where(late == late_here, 0, SIDE) + owner // SIDE

            @pl.when(early == early_here)
            def _():
                keep[slot] = block

            @pl.when(early != early_here)
            def _():
                give[slot] = block


def run_grads(sc, recv, other, scale, w_in, w_out):
    vmem = pl.BlockSpec(memory_space=pltpu.VMEM)
    eight = jax.ShapeDtypeStruct((DP // 2, OUT_ROWS, 2 * HID), BF16)
    return pl.pallas_call(
        grads_kernel,
        in_specs=[pl.BlockSpec(memory_space=pltpu.SMEM)] + [vmem] * 5,
        out_specs=[vmem] * 2,
        out_shape=[eight, eight],
        compiler_params=SMALL,
    )(sc, recv, other, scale, w_in, w_out)


def sum_over_dp(keep, give):
    add = lambda a, b: (a.astype(F32) + b.astype(F32)).astype(BF16)
    trade = lambda v, by: lax.ppermute(
        v,
        ("dp", "mp"),
        [(z * MP + j, (z ^ by[j % 2]) * MP + j) for z in range(DP) for j in range(MP)],
    )
    value = add(keep, trade(give, (1, 2)))
    value = add(value[:SIDE], trade(value[SIDE:], (2, 1)))
    here = lax.axis_index("dp") // SIDE
    block = lambda ahead: lax.dynamic_index_in_dim(
        value, (here + ahead) % SIDE, 0, keepdims=False
    )
    total = block(0).astype(F32)
    for ahead in range(1, SIDE):
        pairs = [(z, (z + ahead * SIDE) % DP) for z in range(DP)]
        total = total + lax.ppermute(block(ahead), "dp", pairs).astype(F32)
    return total.astype(BF16)


def shards(images, token_grads, counts, dw_kernel, ln_gain, w_in, w_out, layer_scale):
    s = lax.axis_index("section")
    j = lax.axis_index("mp")
    chip, core = j // 2, j % 2
    w_in, w_out = w_in[0], w_out[0]

    up = [(i, (i + 2) % MP) for i in range(MP)]
    down = [(i, (i - 2) % MP) for i in range(MP)]
    swap = [(i, i ^ 1) for i in range(MP)]
    move = lambda v, pairs: lax.ppermute(v, "mp", pairs)
    own = jnp.concatenate(
        [jnp.concatenate([w_in[:HALF_C], w_in[HALF_C:]], axis=1), w_out], axis=0
    )
    sample, image = chip // 2, chip % 2
    live = (image < lax.dynamic_index_in_dim(counts, sample, 0, keepdims=False)).astype(BF16)
    one = lambda v: (
        lax.dynamic_index_in_dim(
            v.reshape((CHIPS,) + v.shape[2:]), chip, 0, keepdims=False
        )
        * live
    ).transpose(1, 0, 2).reshape(TOK, C)

    x, g = one(images), one(token_grads)
    params = jnp.concatenate(
        [
            dw_kernel.reshape(TAP_ROWS, C),
            ln_gain,
            layer_scale,
            1.0 / ln_gain,
            jnp.zeros((PARAM_ROWS - TAP_ROWS - 3, C), F32),
        ]
    )
    around = [(i, (i + 2 - 4 * (i % 2)) % MP) for i in range(MP)]
    counter = [(i, (i - 2 + 4 * (i % 2)) % MP) for i in range(MP)]
    first = move(own, around)
    first, own, x, g, params = lax.optimization_barrier((first, own, x, g, params))
    second = move(own, counter)
    third = move(first, around)

    active = [(s == block).astype(jnp.int32)[None] for block in range(DEPTH)]
    send = lambda v, source, to: lax.ppermute(v, "section", [(source, to)])

    result = call_block(
        forward_body,
        active[0],
        dict(x=x, params=params),
        [own, first],
        [0, 1],
        dict(normed=WIDE, sums=SUMS),
    )
    normed = result["normed"]
    swap_own, swap_first, sums = lax.optimization_barrier((own, first, result["sums"]))
    result = call_block(
        forward_body,
        active[0],
        dict(normed_in=normed, sums_in=sums),
        [second, third],
        [0, 1],
        dict(part=WIDE),
    )
    swap_second, swap_third, part = lax.optimization_barrier((second, third, result["part"]))
    result = call_block(
        join_body,
        active[0],
        dict(x=x, params=params, mine=part, other=move(part, swap)),
        [],
        [],
        dict(out=WIDE),
    )
    out = result["out"]

    weights = [own, first, move(swap_own, swap), move(swap_first, swap)]
    weights += [second, third, move(swap_second, swap), move(swap_third, swap)]
    places = list(range(MP))
    normed_of, saved = [normed], [None]
    for block in range(1, DEPTH - 1):
        result = call_block(
            forward_body,
            active[block],
            dict(x=send(out, block - 1, block), params=params),
            weights,
            places,
            dict(out=WIDE, normed=WIDE, rstd=RSTD, slope=SLOPE),
        )
        out = result["out"]
        normed_of.append(result["normed"])
        saved.append(result)
    result = call_block(
        turn_body,
        active[DEPTH - 1],
        dict(x=send(out, DEPTH - 2, DEPTH - 1), g=g, params=params),
        weights,
        places,
        dict(out=WIDE, normed=WIDE),
    )
    normed_of.append(result["normed"])
    g_of = [g]
    for block in range(DEPTH - 2, 0, -1):
        g = send(result["out"], block + 1, block)
        g_of.append(g)
        kept = saved[block]
        result = call_block(
            backward_body,
            active[block],
            dict(
                g=g,
                params=params,
                normed_in=kept["normed"],
                rstd_in=kept["rstd"],
                slope_in=kept["slope"],
            ),
            weights,
            places,
            dict(out=WIDE),
        )
    g_of.append(send(result["out"], 1, 0))

    pick = lambda values: lax.select_n(s, *values)
    mine = jnp.stack([pick(normed_of), pick(g_of[::-1])])
    mine = jnp.where(core == 0, mine[:, :HALF], mine[:, HALF:]).reshape(TOK, C)
    recv = lax.all_to_all(
        jnp.broadcast_to(mine[None], (CHIPS, TOK, C)),
        "mp",
        0,
        0,
        axis_index_groups=[list(range(0, MP, 2)), list(range(1, MP, 2))],
        tiled=True,
    )
    other = move(recv, swap)
    z = lax.axis_index("dp")
    low, high = z % 2, z % SIDE // 2
    place = [jnp.where(core == 0, low, high), jnp.where(core == 0, high, low), core]
    place = jnp.stack([jnp.asarray(v, jnp.int32) for v in place])
    total = sum_over_dp(*run_grads(place, recv, other, layer_scale, w_in, w_out))
    return total[None, :, :HID], total[None, :, HID:]


def solution(mesh):
    return jax.shard_map(
        shards,
        mesh=mesh,
        in_specs=(
            P("dp", None, None, None, None),
            P("dp", None, None, None, None),
            P("dp"),
            P("section", None, None, None),
            P("section", None),
            P("section", None, "mp"),
            P("section", "mp", None),
            P("section", None),
        ),
        out_specs=(P("section", "dp", "mp"), P("section", "dp", "mp")),
        check_vma=False,
    )
```
